128 devices in a mesh: grp: 16 (over y, z), tp: 8 (over x, core).
Axes of the slice: x: 4, y: 4, z: 4, core: 2. Of those that a mesh axis runs over, the one named last changes fastest.
Arguments:
- queries: bfloat16 [2, 512, 128, 576], P(None, 'grp', 'tp'), may hold values from -48 to 48
- new_latent: bfloat16 [2, 512, 576], P(None, 'grp'), may hold values from -7 to 7
- latent_cache: bfloat16 [327680, 576], P('grp'), may hold values from -8 to 8
- tables: int32 [512, 10], P('grp'), may hold values from 0 to 319, as said below
- context_len: int32 [256], replicated, may hold values from 213 to 640, as said below
- group_rows: int32 [16], replicated, may hold values from 1 to 32, 256 in all
- request_order: int32 [256], replicated, may hold values from 0 to 255, each once
- residual: bfloat16 [2, 256, 7168], P(None, None, 'grp'), may hold values from -24 to 24
- value_up: bfloat16 [128, 512, 128], P('tp'), may hold values from -4 to 4
- out_proj: bfloat16 [16384, 7168], P('tp', 'grp'), may hold values from -0.046875 to 0.046875
- norm_gain: bfloat16 [7168], P('grp'), may hold values from 0.099609375 to 1.8984375
- gate_proj: bfloat16 [7168, 18432], P('grp', 'tp'), may hold values from -0.0625 to 0.0625
- up_proj: bfloat16 [7168, 18432], P('grp', 'tp'), may hold values from -0.0625 to 0.0625
- down_proj: bfloat16 [18432, 7168], P('tp', 'grp'), may hold values from -0.046875 to 0.046875
Outputs:
- layer_out: bfloat16 [2, 256, 7168], P(None, 'tp', 'grp')
The draws below stay inside these ranges and needn't reach their ends.
Inputs may be any that keep to these rules, and one draw needn't show every extreme that they name: `tables`: within each group all block ids of its 32 slots are distinct; a context fills its slot's blocks from the first on. `context_len`: one request has a context of exactly 640. `group_rows`: sums to 256; some group has exactly 32 requests; the live requests of group g sit in its first group_rows[g] slots. `request_order`: each position is taken by exactly one request.
All inputs are finite; a program needn't handle non-finite values.
Results may differ from the reference program's by a relative error of at most 0.009.
Values may be sent and summed in bfloat16 or wider, within the bound.
A program may use at most 192 MiB of HBM per device.

```python
import math
import jax
import jax.numpy as jnp
import numpy as np
from jax import lax

D = 7168
FF = 18432
H = 128
KV_RANK = 512
VH = 128
BLOCK = 64
GRPS = 16
SLOTS = 32
REQS = 256
MAXLEN = 640
POOL = 320
KDIM = 576


def block_tables(key):
    subkey = jax.random.fold_in(key, 11)
    group_keys = jax.random.split(subkey, GRPS)
    perms = jax.vmap(lambda one_key: jax.random.permutation(one_key, POOL))(group_keys)
    return perms.reshape(GRPS * SLOTS, POOL // SLOTS).astype(jnp.int32)


def base_cache(key):
    subkey = jax.random.fold_in(key, 13)
    return jax.random.truncated_normal(subkey, -6.0, 6.0, (GRPS * POOL * BLOCK, KDIM), jnp.float32)


def shared_dirs(key):
    subkey = jax.random.fold_in(key, 14)
    return jax.random.truncated_normal(subkey, -6.0, 6.0, (2, GRPS * SLOTS, KDIM), jnp.float32)


def draw_tables(key, part):
    return block_tables(key)


def draw_latent_cache(key, part):
    base_draw = base_cache(key)
    return base_draw.astype(jnp.bfloat16)


def draw_queries(key, part):
    shared_dir = shared_dirs(key)
    key = jax.random.fold_in(key, 22)
    shape = (2, GRPS * SLOTS, H, KDIM)
    own_part = jax.random.truncated_normal(key, -6.0, 6.0, shape, jnp.float32)
    mixed_query = 0.6 * own_part + 0.8 * shared_dir[:, :, None, :]
    return mixed_query.astype(jnp.bfloat16)


def draw_new_latent(key, part):
    shared_dir = shared_dirs(key)
    key = jax.random.fold_in(key, 23)
    shape = (2, GRPS * SLOTS, KDIM)
    fresh = jax.random.truncated_normal(key, -6.0, 6.0, shape, jnp.float32)
    return (0.15 * shared_dir + 0.9 * fresh).astype(jnp.bfloat16)


def draw_context_len(key, part):
    key = jax.random.fold_in(key, 24)
    first_key, second_key = jax.random.split(key)
    lengths = jax.random.randint(first_key, (REQS,), MAXLEN // 3, MAXLEN + 1)
    chosen = jax.random.randint(second_key, (), 0, REQS)
    return lengths.at[chosen].set(MAXLEN).astype(jnp.int32)


def draw_residual(key, part):
    key = jax.random.fold_in(key, 25)
    first_key, second_key, third_key = jax.random.split(key, 3)
    rising = 3.0 ** (0.5 * jnp.arange(D, dtype=jnp.float32) / D)
    normal_part = jax.random.truncated_normal(first_key, -4.0, 4.0, (2, REQS, D), jnp.float32)
    row_scale = jnp.exp(jax.random.uniform(second_key, (2, REQS, 1), jnp.float32, jnp.log(0.3), jnp.log(3.0)))
    col_scale = jnp.exp(jax.random.uniform(third_key, (D,), jnp.float32, jnp.log(0.35), jnp.log(1.1))) * rising
    return (normal_part * row_scale * col_scale).astype(jnp.bfloat16)


def levels(key, extent, cuts, least, high):
    def one(dim, shards_of):
        steps = jax.random.uniform(jax.random.fold_in(jax.random.fold_in(key, 6), dim), (shards_of,), jnp.float32, least / len(cuts), high / len(cuts))
        return jnp.repeat(jnp.exp(steps), extent[dim] // shards_of).reshape((-1,) + (1,) * (len(extent) - dim - 1))

    loudness = one(*cuts[0])
    for cut in cuts[1:]:
        loudness = loudness * one(*cut)
    return loudness


def split_up(count, total, bound, skew):
    portions = [(1 << 20) // math.isqrt(rank ** skew) + 1 for rank in range(2, count + 1)]
    rest, counts = total - bound - (count - 1), [1] * (count - 1)
    while rest > 0:
        free = [i for i in range(count - 1) if counts[i] < bound]
        mass, budget = sum([portions[i] for i in free]), rest
        for i in free:
            addition = min(bound - counts[i], max(1, budget * portions[i] // mass), rest)
            counts[i] = counts[i] + addition
            rest = rest - addition
    return np.array([bound] + counts)


def ragged(own_key, number_of, total, most, skew):
    if number_of == 2:
        one = jax.random.randint(own_key, (), max(1, total - most), min(most, total - 1) + 1)
        return jnp.stack([one, total - one])
    sizes = jnp.asarray(split_up(number_of, total, most, skew), jnp.int32)
    pairs = (number_of - 1) // 2
    source_of, sink = sizes[1:1 + 2 * pairs:2], sizes[2:2 + 2 * pairs:2]
    margin = jnp.minimum(source_of - 1, most - sink)
    passed = jax.random.randint(jax.random.fold_in(own_key, 1), (pairs,), 0, 1 << 20) % (margin + 1)
    sizes = sizes.at[1:1 + 2 * pairs:2].set(source_of - passed).at[2:2 + 2 * pairs:2].set(sink + passed)
    return sizes[jax.random.permutation(jax.random.fold_in(own_key, 2), number_of)]


def normal_values(stream_key, extent, scale, bound, cuts=(), kind=jnp.bfloat16):
    array = scale * jax.random.normal(stream_key, extent, jnp.float32)
    if cuts:
        array = array * levels(stream_key, extent, cuts, -0.22, 0.18)
    return jnp.clip(array, -bound, bound).astype(kind)


def setup_inputs(seed: int = 0) -> dict:
    arg_keys = jax.random.split(jax.random.key(seed), 15)
    queries = draw_queries(jax.random.fold_in(arg_keys[14], 71), 0)
    new_latent = draw_new_latent(jax.random.fold_in(arg_keys[14], 71), 0)
    latent_cache = draw_latent_cache(jax.random.fold_in(arg_keys[14], 71), 0)
    tables = draw_tables(jax.random.fold_in(arg_keys[14], 71), 0)
    context_len = draw_context_len(jax.random.fold_in(arg_keys[14], 71), 0)
    group_rows = ragged(arg_keys[5], GRPS, REQS, SLOTS, 2).astype(jnp.int32)
    request_order = jax.random.permutation(arg_keys[6], REQS).astype(jnp.int32)
    residual = draw_residual(jax.random.fold_in(arg_keys[14], 71), 0)
    value_up = normal_values(arg_keys[8], (H, KV_RANK, VH), 0.25, 4.0, ((0, 8),))
    out_proj = normal_values(arg_keys[9], (H * VH, D), (H * VH) ** -0.5, 0.046875, ((0, 8), (1, 16)))
    norm_gain = jnp.clip(1.0 + 0.18 * jax.random.normal(arg_keys[10], (D,), jnp.float32), 0.099609375, 1.8984375).astype(jnp.bfloat16)
    gate_proj = normal_values(arg_keys[11], (D, FF), D ** -0.5, 0.0625, ((0, 16), (1, 8)))
    up_proj = normal_values(arg_keys[12], (D, FF), D ** -0.5, 0.0625, ((0, 16), (1, 8)))
    down_proj = normal_values(arg_keys[13], (FF, D), FF ** -0.5, 0.046875, ((0, 8), (1, 16)))
    return {"queries": queries, "new_latent": new_latent, "latent_cache": latent_cache, "tables": tables, "context_len": context_len, "group_rows": group_rows, "request_order": request_order, "residual": residual, "value_up": value_up, "out_proj": out_proj, "norm_gain": norm_gain, "gate_proj": gate_proj, "up_proj": up_proj, "down_proj": down_proj}


score_scale = 192.0 ** (-0.5)

def slot_positions(group_rows, request_order, slot_count):
    group_ends = jnp.cumsum(group_rows).astype(jnp.int32)
    group_starts = (group_ends - group_rows).astype(jnp.int32)
    group_of = lax.optimization_barrier(jnp.sum((request_order[:, None] >= group_ends[None, :]).astype(jnp.int32), axis=1)).astype(jnp.int32)
    in_group = group_of[:, None] == jnp.arange(group_rows.shape[0], dtype=jnp.int32)[None, :]
    first_slot = lax.optimization_barrier(jnp.sum(jnp.where(in_group, group_starts[None, :], 0), axis=1)).astype(jnp.int32)
    return (group_of * slot_count + request_order - first_slot).astype(jnp.int32)

def reference(queries, new_latent, latent_cache, tables, context_len, group_rows, request_order, residual, value_up, out_proj, norm_gain, gate_proj, up_proj, down_proj):
    slot_index = slot_positions(group_rows, request_order, SLOTS)
    all_slots = jnp.arange(GRPS * SLOTS, dtype=jnp.int32)
    matches = slot_index[None, :] == all_slots[:, None]
    slot_len = lax.optimization_barrier(jnp.sum(jnp.where(matches, context_len[None, :], 0), axis=1)).astype(jnp.int32)
    positions = jnp.arange(MAXLEN, dtype=jnp.int32)
    offsets = jnp.arange(BLOCK, dtype=jnp.int32)
    visible_new = jnp.arange(2, dtype=jnp.int32)[None, :] <= jnp.arange(2, dtype=jnp.int32)[:, None]
    value_float = value_up.astype(jnp.float32)

    def one_slot(packed):
        slot_id, query_rows, fresh_rows, table_row, length = packed
        group_base = slot_id // SLOTS * POOL
        token_rows = ((group_base + table_row)[:, None] * BLOCK + offsets[None, :]).reshape(-1).astype(jnp.int32)
        key_rows = latent_cache[token_rows].astype(jnp.float32)
        query_float = query_rows.astype(jnp.float32)
        fresh_float = fresh_rows.astype(jnp.float32)
        cached = jnp.einsum('phk,tk->pht', query_float, key_rows) * score_scale
        cached = jnp.where((positions < length)[None, None, :], cached, -jnp.inf)
        current = jnp.einsum('phk,nk->phn', query_float, fresh_float) * score_scale
        current = jnp.where(visible_new[:, None, :], current, -jnp.inf)
        scores = jnp.concatenate([cached, current], axis=2)
        largest = lax.optimization_barrier(jnp.max(scores, axis=2, keepdims=True))
        expo = jnp.exp(scores - largest)
        weights = lax.optimization_barrier((expo / lax.optimization_barrier(jnp.sum(expo, axis=2, keepdims=True))).astype(jnp.bfloat16)).astype(jnp.float32)
        mixed = jnp.einsum('pht,tr->phr', weights[..., :MAXLEN], key_rows[:, :KV_RANK])
        mixed = mixed + jnp.einsum('phn,nr->phr', weights[..., MAXLEN:], fresh_float[:, :KV_RANK])
        latent_out = lax.optimization_barrier(mixed.astype(jnp.bfloat16)).astype(jnp.float32)
        heads_out = jnp.einsum('phr,hrv->phv', latent_out, value_float).astype(jnp.bfloat16)
        return heads_out.reshape(2, H * VH)
    per_slot = lax.map(one_slot, (all_slots, jnp.swapaxes(queries, 0, 1), jnp.swapaxes(new_latent, 0, 1), tables, slot_len))
    gathered = jnp.swapaxes(per_slot[slot_index], 0, 1).reshape(2 * REQS, H * VH)
    attention = jnp.dot(gathered, out_proj, preferred_element_type=jnp.float32).reshape(2, REQS, D)
    stream = residual.astype(jnp.float32) + attention
    inverse_rms = lax.rsqrt(lax.optimization_barrier(jnp.sum(stream * stream, axis=2)) / D + 1e-06)
    normed = (stream * inverse_rms[..., None] * norm_gain.astype(jnp.float32)).astype(jnp.bfloat16).reshape(2 * REQS, D)
    gate_part = jnp.dot(normed, gate_proj, preferred_element_type=jnp.float32)
    up_part = jnp.dot(normed, up_proj, preferred_element_type=jnp.float32)
    hidden = (jax.nn.silu(gate_part) * up_part).astype(jnp.bfloat16)
    result = stream + jnp.dot(hidden, down_proj, preferred_element_type=jnp.float32).reshape(2, REQS, D)
    return result.astype(jnp.bfloat16)
```

```python
import functools

import jax
import jax.numpy as jnp
from jax import lax
from jax.experimental import pallas as pl
from jax.experimental.pallas import tpu as pltpu
from jax.sharding import PartitionSpec as P

D = 7168
SLOTS = 32
BLOCKS = 10
BLOCK = 64
SPAN = BLOCKS * BLOCK
HEADS = 16
KDIM = 576
RANK = 512
VH = 128
GRPS = 16
REQS = 256

score_scale = 192.0 ** (-0.5)
NT = (((1,), (1,)), ((), ()))


def attention_kernel(
    tables, order, ctx, rows, q_ref, new_ref, cache, vup_ref, out_ref, raw, keys, lat, fresh_all, lens, sems
):
    group = lax.axis_index("grp")

    def add_rows(j, total):
        return total + jnp.where(j < group, rows[j], 0)

    start = lax.fori_loop(0, GRPS, add_rows, 0)
    live = rows[group]

    def clear(i, carry):
        lens[i] = 0
        return carry

    lax.fori_loop(0, SLOTS + 1, clear, 0)

    def put_len(r, carry):
        where = order[r] - start
        inside = jnp.logical_and(where >= 0, where < live)
        lens[jnp.where(inside, where, SLOTS)] = ctx[r]
        return carry

    lax.fori_loop(0, REQS, put_len, 0, unroll=8)

    def copies(pair, buf, action):
        for k in range(2):
            slot = pair * 2 + k
            count = jnp.where(slot < live, (lens[slot] + BLOCK - 1) // BLOCK, 0)
            for j in range(BLOCKS):

                @pl.when(j < count)
                def _():
                    block = tables[slot * BLOCKS + j]
                    first = pl.multiple_of((block // 2) * (2 * BLOCK), 2 * BLOCK)
                    action(
                        pltpu.make_async_copy(
                            cache.at[:, pl.ds(first, 2 * BLOCK)],
                            raw.at[buf, k * BLOCKS + j],
                            sems.at[buf, k * BLOCKS + j],
                        )
                    )

    pairs = (live + 1) // 2
    raw[...] = jnp.zeros_like(raw)
    copies(0, 0, lambda c: c.start())
    lat[...] = jnp.zeros_like(lat)
    fresh_all[...] = new_ref[...].astype(jnp.float32)
    low = lax.broadcasted_iota(jnp.int32, (KDIM, 2 * BLOCK), 1) < BLOCK
    position = lax.broadcasted_iota(jnp.int32, (2 * HEADS, SPAN), 1)
    step_of = lax.broadcasted_iota(jnp.int32, (2 * HEADS, 1), 0) // HEADS

    def one_pair(pair, carry):
        buf = lax.rem(pair, 2)
        copies(pair, buf, lambda c: c.wait())

        @pl.when(pair + 1 < pairs)
        def _():
            copies(pair + 1, 1 - buf, lambda c: c.start())

        for k in range(2):
            slot = pair * 2 + k
            for j in range(BLOCKS // 2):
                odd_a = lax.rem(tables[slot * BLOCKS + 2 * j], 2)
                odd_b = lax.rem(tables[slot * BLOCKS + 2 * j + 1], 2)
                a = raw[buf, k * BLOCKS + 2 * j]
                b = raw[buf, k * BLOCKS + 2 * j + 1]
                a = pltpu.roll(a, odd_a * BLOCK, 1)
                b = pltpu.roll(b, (1 - odd_b) * BLOCK, 1)
                keys[k, :, j * 128 : (j + 1) * 128] = jnp.where(low, a, b)
        for k in range(2):
            slot = pair * 2 + k
            q = q_ref[:, slot].reshape(2 * HEADS, KDIM)
            fresh_float = [fresh_all[t, pl.ds(slot, 1), :] for t in range(2)]
            scores = jnp.dot(q, keys[k], preferred_element_type=jnp.float32) * score_scale
            scores = jnp.where(position < lens[slot], scores, -jnp.inf)
            q_float = q.astype(jnp.float32)
            now = jnp.sum(q_float * fresh_float[0], axis=1, keepdims=True) * score_scale
            later = jnp.sum(q_float * fresh_float[1], axis=1, keepdims=True) * score_scale
            later = jnp.where(step_of == 1, later, -jnp.inf)
            largest = jnp.maximum(jnp.max(scores, axis=1, keepdims=True), jnp.maximum(now, later))
            expo = jnp.exp(scores - largest)
            now = jnp.exp(now - largest)
            later = jnp.exp(later - largest)
            inverse = 1.0 / (jnp.sum(expo, axis=1, keepdims=True) + now + later)
            mixed = lax.dot_general(
                expo.astype(jnp.bfloat16), keys[k, :RANK, :], NT, preferred_element_type=jnp.float32
            )
            mixed = mixed + now * fresh_float[0][:, :RANK] + later * fresh_float[1][:, :RANK]
            lat[slot] = mixed * inverse
        return carry

    lax.fori_loop(0, pairs, one_pair, 0)

    for h in range(HEADS):
        both = jnp.concatenate([lat[:, h, :], lat[:, HEADS + h, :]], axis=0).astype(jnp.bfloat16)
        value = jnp.dot(both, vup_ref[h], preferred_element_type=jnp.float32).astype(jnp.bfloat16)
        out_ref[0, :, h * VH : (h + 1) * VH] = value[:SLOTS]
        out_ref[1, :, h * VH : (h + 1) * VH] = value[SLOTS:]


def attend(queries, new_latent, latent_cache, tables, context_len, group_rows, request_order, value_up):
    smem = pl.BlockSpec(memory_space=pltpu.SMEM)
    vmem = pl.BlockSpec(memory_space=pltpu.VMEM)
    return pl.pallas_call(
        attention_kernel,
        out_shape=jax.ShapeDtypeStruct((2, SLOTS, HEADS * VH), jnp.bfloat16),
        in_specs=[smem] * 4 + [vmem, vmem, pl.BlockSpec(memory_space=pl.ANY), vmem],
        out_specs=vmem,
        scratch_shapes=[
            pltpu.VMEM((2, 2 * BLOCKS, KDIM, 2 * BLOCK), jnp.bfloat16),
            pltpu.VMEM((2, KDIM, SPAN), jnp.bfloat16),
            pltpu.VMEM((SLOTS, 2 * HEADS, RANK), jnp.float32),
            pltpu.VMEM((2, SLOTS, KDIM), jnp.float32),
            pltpu.SMEM((SLOTS + 1,), jnp.int32),
            pltpu.SemaphoreType.DMA((2, 2 * BLOCKS)),
        ],
        compiler_params=pltpu.CompilerParams(vmem_limit_bytes=40 << 20),
    )(
        tables.reshape(-1),
        request_order,
        context_len,
        group_rows,
        queries,
        new_latent,
        latent_cache.T,
        value_up,
    )


def slot_positions(group_rows, request_order, slot_count):
    group_ends = jnp.cumsum(group_rows)
    group_starts = group_ends - group_rows
    group_of = jnp.sum((request_order[:, None] >= group_ends[None, :]).astype(jnp.int32), axis=1)
    in_group = group_of[:, None] == jnp.arange(group_rows.shape[0], dtype=jnp.int32)[None, :]
    first_slot = jnp.sum(jnp.where(in_group, group_starts[None, :], 0), axis=1)
    return group_of * slot_count + request_order - first_slot


def shards(
    queries,
    new_latent,
    latent_cache,
    tables,
    context_len,
    group_rows,
    request_order,
    residual,
    value_up,
    out_proj,
    norm_gain,
    gate_proj,
    up_proj,
    down_proj,
):
    slot_count = tables.shape[0]
    requests = request_order.shape[0]
    tp_count = lax.axis_size("tp")
    my_requests = requests // tp_count
    heads_out = attend(
        queries, new_latent, latent_cache, tables, context_len, group_rows, request_order, value_up
    )
    slot_index = slot_positions(group_rows, request_order, slot_count)

    def project(portion):
        return jnp.einsum("psv,vd->psd", portion, out_proj, preferred_element_type=jnp.float32)

    def finish(head_block, residual_block):
        step_count = head_block.shape[0]
        partials = project(lax.all_gather(head_block, "grp", axis=1, tiled=True))
        partials = jnp.take(partials, slot_index, axis=1)
        attention = lax.psum(partials, "tp")
        stream = residual_block.astype(jnp.float32) + attention
        squares = lax.psum(jnp.sum(stream * stream, axis=2), "grp")
        inverse_rms = lax.rsqrt(squares / D + 1e-06)
        normed = (stream * inverse_rms[..., None] * norm_gain.astype(jnp.float32)).astype(
            jnp.bfloat16
        )
        normed = jnp.swapaxes(normed, 0, 1).reshape(requests * step_count, -1)
        gate_local = jnp.dot(normed, gate_proj, preferred_element_type=jnp.float32)
        up_local = jnp.dot(normed, up_proj, preferred_element_type=jnp.float32)
        gate_part, up_part = lax.psum((gate_local, up_local), "grp")
        hidden = (jax.nn.silu(gate_part) * up_part).astype(jnp.bfloat16)
        reduced = lax.psum_scatter(
            jnp.dot(hidden, down_proj, preferred_element_type=jnp.float32).astype(jnp.bfloat16),
            "tp",
            scatter_dimension=0,
            tiled=True,
        ).astype(jnp.float32)
        reduced = jnp.swapaxes(reduced.reshape(my_requests, step_count, -1), 0, 1)
        mine = lax.dynamic_slice_in_dim(stream, lax.axis_index("tp") * my_requests, my_requests, 1)
        return (mine + reduced).astype(jnp.bfloat16)

    layer_out = jnp.concatenate(
        [
            finish(heads_out[step_index : step_index + 1], residual[step_index : step_index + 1])
            for step_index in range(2)
        ],
        axis=0,
    )
    return layer_out


def solution(mesh):
    placed = (
        P(None, "grp", "tp", None),
        P(None, "grp", None),
        P("grp", None),
        P("grp", None),
        P(),
        P(),
        P(),
        P(None, None, "grp"),
        P("tp", None, None),
        P("tp", "grp"),
        P("grp"),
        P("grp", "tp"),
        P("grp", "tp"),
        P("tp", "grp"),
    )
    return jax.shard_map(
        shards, mesh=mesh, in_specs=placed, out_specs=P(None, "tp", "grp"), check_vma=False
    )
```

```python
import jax
import jax.numpy as jnp
from jax import lax
from jax.experimental import pallas as pl
from jax.experimental.pallas import tpu as pltpu
from jax.sharding import PartitionSpec as P

D = 7168
SLOTS = 32
BLOCKS = 10
BLOCK = 64
SPAN = BLOCKS * BLOCK
HEADS = 16
KDIM = 576
RANK = 512
VH = 128
GRPS = 16
REQS = 256

score_scale = 192.0 ** (-0.5)
NT = (((1,), (1,)), ((), ()))


def attention_kernel(
    tables, order, ctx, rows, q_ref, new_ref, cache, vup_ref, out_ref, raw, keys, lat, fresh_all, lens, sems
):
    group = lax.axis_index("grp")

    def add_rows(j, total):
        return total + jnp.where(j < group, rows[j], 0)

    start = lax.fori_loop(0, GRPS, add_rows, 0)
    live = rows[group]

    def clear(i, carry):
        lens[i] = 0
        return carry

    lax.fori_loop(0, SLOTS + 1, clear, 0)

    def put_len(r, carry):
        where = order[r] - start
        inside = jnp.logical_and(where >= 0, where < live)
        lens[jnp.where(inside, where, SLOTS)] = ctx[r]
        return carry

    lax.fori_loop(0, REQS, put_len, 0, unroll=8)

    def copies(pair, buf, action):
        for k in range(2):
            slot = pair * 2 + k
            count = jnp.where(slot < live, (lens[slot] + BLOCK - 1) // BLOCK, 0)
            for j in range(BLOCKS):

                @pl.when(j < count)
                def _():
                    block = tables[slot * BLOCKS + j]
                    first = pl.multiple_of((block // 2) * (2 * BLOCK), 2 * BLOCK)
                    action(
                        pltpu.make_async_copy(
                            cache.at[:, pl.ds(first, 2 * BLOCK)],
                            raw.at[buf, k * BLOCKS + j],
                            sems.at[buf, k * BLOCKS + j],
                        )
                    )

    pairs = (live + 1) // 2
    raw[...] = jnp.zeros_like(raw)
    copies(0, 0, lambda c: c.start())
    lat[...] = jnp.zeros_like(lat)
    fresh_all[...] = new_ref[...].astype(jnp.float32)
    low = lax.broadcasted_iota(jnp.int32, (KDIM, 2 * BLOCK), 1) < BLOCK
    position = lax.broadcasted_iota(jnp.int32, (2 * HEADS, SPAN), 1)
    step_of = lax.broadcasted_iota(jnp.int32, (2 * HEADS, 1), 0) // HEADS

    def one_pair(pair, carry):
        buf = lax.rem(pair, 2)
        copies(pair, buf, lambda c: c.wait())

        @pl.when(pair + 1 < pairs)
        def _():
            copies(pair + 1, 1 - buf, lambda c: c.start())

        for k in range(2):
            slot = pair * 2 + k
            for j in range(BLOCKS // 2):
                odd_a = lax.rem(tables[slot * BLOCKS + 2 * j], 2)
                odd_b = lax.rem(tables[slot * BLOCKS + 2 * j + 1], 2)
                a = raw[buf, k * BLOCKS + 2 * j]
                b = raw[buf, k * BLOCKS + 2 * j + 1]
                a = pltpu.roll(a, odd_a * BLOCK, 1)
                b = pltpu.roll(b, (1 - odd_b) * BLOCK, 1)
                keys[k, :, j * 128 : (j + 1) * 128] = jnp.where(low, a, b)
        for k in range(2):
            slot = pair * 2 + k
            q = q_ref[:, slot].reshape(2 * HEADS, KDIM)
            fresh_float = [fresh_all[t, pl.ds(slot, 1), :] for t in range(2)]
            scores = jnp.dot(q, keys[k], preferred_element_type=jnp.float32) * score_scale
            scores = jnp.where(position < lens[slot], scores, -jnp.inf)
            q_float = q.astype(jnp.float32)
            now = jnp.sum(q_float * fresh_float[0], axis=1, keepdims=True) * score_scale
            later = jnp.sum(q_float * fresh_float[1], axis=1, keepdims=True) * score_scale
            later = jnp.where(step_of == 1, later, -jnp.inf)
            largest = jnp.maximum(jnp.max(scores, axis=1, keepdims=True), jnp.maximum(now, later))
            expo = jnp.exp(scores - largest)
            now = jnp.exp(now - largest)
            later = jnp.exp(later - largest)
            inverse = 1.0 / (jnp.sum(expo, axis=1, keepdims=True) + now + later)
            mixed = lax.dot_general(
                expo.astype(jnp.bfloat16), keys[k, :RANK, :], NT, preferred_element_type=jnp.float32
            )
            mixed = mixed + now * fresh_float[0][:, :RANK] + later * fresh_float[1][:, :RANK]
            lat[slot] = mixed * inverse
        return carry

    lax.fori_loop(0, pairs, one_pair, 0)

    for h in range(HEADS):
        both = jnp.concatenate([lat[:, h, :], lat[:, HEADS + h, :]], axis=0).astype(jnp.bfloat16)
        value = jnp.dot(both, vup_ref[h], preferred_element_type=jnp.float32).astype(jnp.bfloat16)
        out_ref[0, :, h * VH : (h + 1) * VH] = value[:SLOTS]
        out_ref[1, :, h * VH : (h + 1) * VH] = value[SLOTS:]


def attend(queries, new_latent, latent_cache, tables, context_len, group_rows, request_order, value_up):
    smem = pl.BlockSpec(memory_space=pltpu.SMEM)
    vmem = pl.BlockSpec(memory_space=pltpu.VMEM)
    return pl.pallas_call(
        attention_kernel,
        out_shape=jax.ShapeDtypeStruct((2, SLOTS, HEADS * VH), jnp.bfloat16),
        in_specs=[smem] * 4 + [vmem, vmem, pl.BlockSpec(memory_space=pl.ANY), vmem],
        out_specs=vmem,
        scratch_shapes=[
            pltpu.VMEM((2, 2 * BLOCKS, KDIM, 2 * BLOCK), jnp.bfloat16),
            pltpu.VMEM((2, KDIM, SPAN), jnp.bfloat16),
            pltpu.VMEM((SLOTS, 2 * HEADS, RANK), jnp.float32),
            pltpu.VMEM((2, SLOTS, KDIM), jnp.float32),
            pltpu.SMEM((SLOTS + 1,), jnp.int32),
            pltpu.SemaphoreType.DMA((2, 2 * BLOCKS)),
        ],
        compiler_params=pltpu.CompilerParams(vmem_limit_bytes=40 << 20),
    )(
        tables.reshape(-1),
        request_order,
        context_len,
        group_rows,
        queries,
        new_latent,
        latent_cache.T,
        value_up,
    )


MESH = pl.DeviceIdType.MESH
WIDE = 512
COLS = 448
FFT = 2304
TAIL = 128
BF16 = jnp.bfloat16
F32 = jnp.float32


def layer_kernel(
    heads,
    order_ref,
    rows_ref,
    residual,
    gain_ref,
    wo_hbm,
    wg_hbm,
    wu_hbm,
    wd_hbm,
    out_ref,
    wo,
    wg,
    wu,
    wd,
    res,
    gathered,
    hiddens,
    select,
    stream,
    part,
    from_core,
    summed,
    from_x,
    normed,
    chunks_a,
    chunks_b,
    relay_a,
    relay_b,
    final_a,
    final_b,
    line_a,
    line_b,
    relay2_a,
    relay2_b,
    final2_a,
    final2_b,
    local_sems,
    send_sems,
    recv_sems,
):
    g, t = lax.axis_index("grp"), lax.axis_index("tp")
    y, z = g // 4, lax.rem(g, 4)
    x, core = t // 2, lax.rem(t, 2)

    def group_at(dy, dz):
        return lax.rem(y + dy + 4, 4) * 4 + lax.rem(z + dz + 4, 4)

    def tp_at(dx):
        return lax.rem(x + dx + 4, 4) * 2 + core

    partner = x * 2 + 1 - core
    used = []

    def remote(src, dst, device):
        i = len(used)
        copy = pltpu.make_async_remote_copy(
            src_ref=src,
            dst_ref=dst,
            send_sem=send_sems.at[i],
            recv_sem=recv_sems.at[i],
            device_id=device,
            device_id_type=MESH,
        )
        copy.start()
        used.append(copy)
        return copy

    local = []

    def bring(src, dst):
        copy = pltpu.make_async_copy(src, dst, local_sems.at[len(local)])
        copy.start()
        local.append(copy)
        return copy

    heads_in = [bring(heads.at[:, :, pl.ds(h * 1024, 1024)], gathered.at[h, g]) for h in range(2)]
    wo_in = bring(wo_hbm, wo)
    res_in = bring(residual, res)
    wg_in = bring(wg_hbm, wg)
    wu_in = bring(wu_hbm, wu)
    wd_in = bring(wd_hbm, wd)

    barrier = pltpu.get_barrier_semaphore()
    greet = [(group_at(dy, dz), t) for dy, dz in ((1, 0), (-1, 0), (0, 1), (0, -1))]
    greet += [(g, tp_at(1)), (g, tp_at(-1)), (g, tp_at(2)), (g, partner)]
    for device in greet:
        pl.semaphore_signal(barrier, inc=1, device_id=device, device_id_type=MESH)
    pl.semaphore_wait(barrier, len(greet))

    def all_gather(bufs):
        def slot(h, da, db):
            return group_at(da, db) if h == 0 else group_at(db, da)

        def send(h, da, db, to_a, to_b, half=None):
            at = slot(h, da, db)
            ref = bufs[h].at[at] if half is None else bufs[h].at[at, half]
            return remote(ref, ref, (slot(h, to_a, to_b), t))

        along = [{}, {}]
        up, down, up2, down2 = [{}, {}], [{}, {}], [{}, {}], [{}, {}]

        def across(h, d):
            up[h][d] = send(h, d, 0, 0, 1)
            down[h][d] = send(h, d, 0, 0, -1)

        def pass_on(h, d):
            up[h][d].wait_recv()
            up2[h][d] = send(h, d, -1, 0, 1, 0)
            down[h][d].wait_recv()
            down2[h][d] = send(h, d, 1, 0, -1, 1)

        for h in range(2):
            along[h]["+"] = send(h, 0, 0, 1, 0)
            along[h]["-"] = send(h, 0, 0, -1, 0)
            across(h, 0)
        for h in range(2):
            along[h]["+"].wait_recv()
            along[h]["++"] = send(h, -1, 0, 1, 0, 0)
            across(h, -1)
            along[h]["-"].wait_recv()
            along[h]["--"] = send(h, 1, 0, -1, 0, 1)
            across(h, 1)
        for h in range(2):
            pass_on(h, 0)
        for h in range(2):
            along[h]["++"].wait_recv()
            along[h]["--"].wait_recv()
            across(h, 2)
        for d in (-1, 1, 2):
            for h in range(2):
                pass_on(h, d)
        for d in (0, -1, 1, 2):
            for h in range(2):
                up2[h][d].wait_recv()
                down2[h][d].wait_recv()

    def scatter_tp(turn):
        to_core = remote(part.at[turn, 1 - core], from_core.at[turn], (g, partner))
        to_core.wait_recv()
        for k in range(4):
            summed[turn, k] = (
                part[turn, core, k].astype(F32) + from_core[turn, k].astype(F32)
            ).astype(BF16)
        moves = []
        for i, dx in enumerate((1, -1, 2)):
            chip = lax.rem(x + dx + 4, 4)
            moves.append(remote(summed.at[turn, chip], from_x.at[turn, i], (g, tp_at(dx))))
        total = summed[turn, x].astype(F32)
        for i, move in enumerate(moves):
            move.wait_recv()
            total = total + from_x[turn, i].astype(F32)
        return total[:, :COLS]

    for copy in heads_in:
        copy.wait()
    all_gather([gathered.at[0], gathered.at[1]])

    spread = lax.broadcasted_iota(jnp.int32, (GRPS, GRPS), 1)
    row_of = lax.broadcasted_iota(jnp.int32, (GRPS, GRPS), 0)
    ends = jnp.sum(jnp.where(spread <= row_of, rows_ref[...], 0), axis=1, keepdims=True)
    starts = jnp.sum(jnp.where(spread < row_of, rows_ref[...], 0), axis=1, keepdims=True)
    order = order_ref[...]
    in_group = jnp.logical_and(order >= starts, order < ends)
    group_id = lax.broadcasted_iota(jnp.int32, (GRPS, REQS), 0)
    at = jnp.sum(jnp.where(in_group, group_id * SLOTS + order - starts, 0), axis=0, keepdims=True)
    matches = lax.broadcasted_iota(jnp.int32, (GRPS * SLOTS, REQS), 0) == at
    select[...] = jnp.where(matches, 1.0, 0.0).astype(BF16)

    wo_in.wait()
    part[:, :, :, :, 384:] = jnp.zeros(part.shape[:-1] + (128,), BF16)
    TN = (((0,), (0,)), ((), ()))
    for s in range(2):
        rows = []
        for q in range(2):
            both = [gathered[h, pl.ds(8 * q, 8), s].reshape(8 * SLOTS, 1024) for h in range(2)]
            value = lax.dot_general(both[0], wo[:, :1024], NT, preferred_element_type=F32)
            value = value + lax.dot_general(both[1], wo[:, 1024:], NT, preferred_element_type=F32)
            rows.append(value.astype(BF16))
        value = jnp.concatenate(rows, axis=0)
        placed = lax.dot_general(select[...], value, TN, preferred_element_type=F32).astype(BF16)
        for k in range(8):
            part[0, k % 2, k // 2, s * 32 : s * 32 + 32, :COLS] = placed[32 * k : 32 * k + 32]
    attention = scatter_tp(0)

    res_in.wait()
    mine = lax.broadcasted_iota(jnp.int32, (32, REQS), 1) == (
        lax.broadcasted_iota(jnp.int32, (32, REQS), 0) + t * 32
    )
    mine = jnp.where(mine, 1.0, 0.0).astype(BF16)
    for s in range(2):
        own = lax.dot_general(mine, res[s], NT, preferred_element_type=F32)
        stream[s * 32 : s * 32 + 32, :] = own + attention[s * 32 : s * 32 + 32]
    here = stream[...]
    squares = jnp.sum(here * here, axis=1, keepdims=True)
    high = squares.astype(BF16)
    low = (squares - high.astype(F32)).astype(BF16)
    lane = lax.broadcasted_iota(jnp.int32, (64, WIDE - COLS), 1)
    extra = jnp.where(lane == 0, high, jnp.where(lane == 1, low, jnp.zeros_like(high)))
    scaled = (here * gain_ref[...].astype(F32)).astype(BF16)
    scaled = jnp.concatenate([scaled, extra], axis=1)
    normed[2 * t] = scaled[:32]
    normed[2 * t + 1] = scaled[32:]

    def pair(index):
        return normed.at[pl.ds(2 * index, 2)]

    moves = [remote(pair(t), pair(t), (g, tp_at(dx))) for dx in (1, -1, 2)]
    moves.append(remote(pair(t), pair(t), (g, partner)))
    shares = []
    for move, dx in zip(moves[:3], (-1, 1, 2)):
        move.wait_recv()
        shares.append(remote(pair(tp_at(dx)), pair(tp_at(dx)), (g, partner)))
    for move in moves[3:] + shares:
        move.wait_recv()
    wg_in.wait()
    wu_in.wait()

    chunks, weight = (chunks_a, chunks_b), (wg, wu)
    relay, final, line = (relay_a, relay_b), (final_a, final_b), (line_a, line_b)
    relay2, final2 = (relay2_a, relay2_b), (final2_a, final2_b)
    cut = (1280, 1152)
    first = (pl.ds(0, 1280), pl.ds(0, 1152))
    second = (pl.ds(1280, 1152), pl.ds(1152, 1152))

    def along(h, d):
        return (group_at(d, 0) if h == 0 else group_at(0, d), t)

    def across(h, d):
        return along(1 - h, d)

    def product(h, i, d):
        blocks = []
        for k in range(4):
            b = lax.rem(y + d + 4, 4) * 4 + k if h == 0 else k * 4 + lax.rem(z + d + 4, 4)
            blocks.append(normed[b])
        rows = jnp.concatenate(blocks, axis=0)
        if h == 0:
            chunks[h][i, :, FFT:] = rows[:, 384:]
        rows = rows[:, :COLS]

        def one(n, carry):
            at = pl.ds(pl.multiple_of(n * 256, 256), 256)
            chunks[h][i, :, at] = jnp.dot(
                rows, weight[h][:, at], preferred_element_type=F32
            ).astype(BF16)
            return carry

        lax.fori_loop(0, FFT // 256, one, 0)

    def add(ref, index, part_cols, other):
        ref[index, :, part_cols] = (
            ref[index, :, part_cols].astype(F32) + other[...].astype(F32)
        ).astype(BF16)

    relays, finals = [None, None], [[], []]
    for h in range(2):
        product(h, 2, 2)
        relays[h] = (
            remote(chunks[h].at[2, :, first[h]], relay[h].at[0, :, first[h]], along(h, 1)),
            remote(chunks[h].at[2, :, second[h]], relay[h].at[1, :, pl.ds(0, 1152)], along(h, -1)),
        )
    for h in range(2):
        product(h, 1, 1)
        finals[h].append(
            remote(chunks[h].at[1, :, second[h]], final[h].at[0, :, second[h]], along(h, 1))
        )
        product(h, 3, -1)
        finals[h].append(
            remote(chunks[h].at[3, :, first[h]], final[h].at[1, :, first[h]], along(h, -1))
        )
    for h in range(2):
        relays[h][0].wait_recv()
        add(chunks[h], 1, first[h], relay[h].at[0, :, first[h]])
        finals[h].append(
            remote(chunks[h].at[1, :, first[h]], final[h].at[0, :, first[h]], along(h, 1))
        )
        relays[h][1].wait_recv()
        add(chunks[h], 3, second[h], relay[h].at[1, :, pl.ds(0, 1152)])
        finals[h].append(
            remote(chunks[h].at[3, :, second[h]], final[h].at[1, :, second[h]], along(h, -1))
        )
    for h in range(2):
        product(h, 0, 0)
    relays, finals2 = [None, None], [[], []]
    for h in range(2):
        for copy in finals[h]:
            copy.wait_recv()
        for k in range(4):
            at = pl.ds(32 * k, 32)
            line[h][k] = (
                chunks[h][0, at, :].astype(F32)
                + final[h][0, at, :].astype(F32)
                + final[h][1, at, :].astype(F32)
            ).astype(BF16)
        spot = z if h == 0 else y

        def place(d):
            return lax.rem(spot + d + 4, 4)

        far, ahead, behind = place(2), place(1), place(-1)
        relays[h] = (
            remote(line[h].at[far, :, first[h]], relay2[h].at[0, :, first[h]], across(h, 1)),
            remote(line[h].at[far, :, second[h]], relay2[h].at[1, :, pl.ds(0, 1152)], across(h, -1)),
        )
        finals2[h].append(
            remote(line[h].at[ahead, :, second[h]], final2[h].at[0, :, second[h]], across(h, 1))
        )
        finals2[h].append(
            remote(line[h].at[behind, :, first[h]], final2[h].at[1, :, first[h]], across(h, -1))
        )
    totals = []
    for h in range(2):
        spot = z if h == 0 else y
        ahead, behind = lax.rem(spot + 1, 4), lax.rem(spot + 3, 4)
        relays[h][0].wait_recv()
        add(line[h], ahead, first[h], relay2[h].at[0, :, first[h]])
        finals2[h].append(
            remote(line[h].at[ahead, :, first[h]], final2[h].at[0, :, first[h]], across(h, 1))
        )
        relays[h][1].wait_recv()
        add(line[h], behind, second[h], relay2[h].at[1, :, pl.ds(0, 1152)])
        finals2[h].append(
            remote(line[h].at[behind, :, second[h]], final2[h].at[1, :, second[h]], across(h, -1))
        )
    for h in range(2):
        for copy in finals2[h]:
            copy.wait_recv()
        spot = z if h == 0 else y
        totals.append(
            line[h][spot].astype(F32) + final2[h][0].astype(F32) + final2[h][1].astype(F32)
        )
    mean = (totals[0][:, FFT + 64 : FFT + 65] + totals[0][:, FFT + 65 : FFT + 66]) / D
    inverse_rms = lax.rsqrt(mean + 1e-06)
    gate = totals[0][:, :FFT] * inverse_rms
    up = totals[1] * inverse_rms
    hidden = (gate / (1.0 + jnp.exp(-gate)) * up).astype(BF16)
    for h in range(2):
        for k in range(2):
            hiddens[h, g, k] = hidden[16 * k : 16 * k + 16, 1152 * h : 1152 * h + 1152]
    all_gather([hiddens.at[0], hiddens.at[1]])

    wd_in.wait()
    for q in range(4):
        both = [hiddens[h, 4 * q : 4 * q + 4].reshape(128, 1152) for h in range(2)]
        value = lax.dot_general(both[0], wd[:, :1152], NT, preferred_element_type=F32)
        value = value + lax.dot_general(both[1], wd[:, 1152:], NT, preferred_element_type=F32)
        value = value.astype(BF16)
        for k in range(2):
            part[1, k, q, :, :COLS] = value[64 * k : 64 * k + 64]
    reduced = scatter_tp(1)
    for s in range(2):
        at = slice(32 * s, 32 * s + 32)
        out_ref[s] = (stream[at, :] + reduced[at]).astype(BF16)
    for copy in used:
        copy.wait_send()


def layer(heads, request_order, group_rows, residual, norm_gain, out_proj, gate_proj, up_proj, down_proj):
    vmem = pl.BlockSpec(memory_space=pltpu.VMEM)
    hbm = pl.BlockSpec(memory_space=pl.ANY)
    copies = 40 + 40 + 4 + 4 + 4 + 3 + 12 + 12
    return pl.pallas_call(
        layer_kernel,
        out_shape=jax.ShapeDtypeStruct((2, 32, COLS), BF16),
        in_specs=[hbm, vmem, vmem, hbm, vmem, hbm, hbm, hbm, hbm],
        out_specs=vmem,
        scratch_shapes=[
            pltpu.VMEM((COLS, 2048), BF16),
            pltpu.VMEM((COLS, FFT), BF16),
            pltpu.VMEM((COLS, FFT), BF16),
            pltpu.VMEM((COLS, FFT), BF16),
            pltpu.VMEM((2, COLS, REQS), BF16),
            pltpu.VMEM((2, GRPS, 2, SLOTS, 1024), BF16),
            pltpu.VMEM((2, GRPS, 2, 16, 1152), BF16),
            pltpu.VMEM((GRPS * SLOTS, REQS), BF16),
            pltpu.VMEM((64, COLS), F32),
            pltpu.VMEM((2, 2, 4, 64, WIDE), BF16),
            pltpu.VMEM((2, 4, 64, WIDE), BF16),
            pltpu.VMEM((2, 4, 64, WIDE), BF16),
            pltpu.VMEM((2, 3, 64, WIDE), BF16),
            pltpu.VMEM((16, 32, WIDE), BF16),
            pltpu.VMEM((4, 128, FFT + TAIL), BF16),
            pltpu.VMEM((4, 128, FFT), BF16),
            pltpu.VMEM((2, 128, 1280), BF16),
            pltpu.VMEM((2, 128, 1152), BF16),
            pltpu.VMEM((2, 128, FFT + TAIL), BF16),
            pltpu.VMEM((2, 128, FFT), BF16),
            pltpu.VMEM((4, 32, FFT + TAIL), BF16),
            pltpu.VMEM((4, 32, FFT), BF16),
            pltpu.VMEM((2, 32, 1280), BF16),
            pltpu.VMEM((2, 32, 1152), BF16),
            pltpu.VMEM((2, 32, FFT + TAIL), BF16),
            pltpu.VMEM((2, 32, FFT), BF16),
            pltpu.SemaphoreType.DMA((7,)),
            pltpu.SemaphoreType.DMA((copies,)),
            pltpu.SemaphoreType.DMA((copies,)),
        ],
        compiler_params=pltpu.CompilerParams(
            collective_id=0, has_side_effects=True, vmem_limit_bytes=56 << 20
        ),
    )(
        heads,
        request_order.reshape(1, REQS),
        group_rows.reshape(1, GRPS),
        jnp.swapaxes(residual, 1, 2),
        norm_gain.reshape(1, COLS),
        out_proj.T,
        gate_proj,
        up_proj,
        down_proj.T,
    )


def shards(
    queries,
    new_latent,
    latent_cache,
    tables,
    context_len,
    group_rows,
    request_order,
    residual,
    value_up,
    out_proj,
    norm_gain,
    gate_proj,
    up_proj,
    down_proj,
):
    heads = attend(
        queries, new_latent, latent_cache, tables, context_len, group_rows, request_order, value_up
    )
    return layer(
        heads,
        request_order,
        group_rows,
        residual,
        norm_gain,
        out_proj,
        gate_proj,
        up_proj,
        down_proj,
    )


def solution(mesh):
    placed = (
        P(None, "grp", "tp", None),
        P(None, "grp", None),
        P("grp", None),
        P("grp", None),
        P(),
        P(),
        P(),
        P(None, None, "grp"),
        P("tp", None, None),
        P("tp", "grp"),
        P("grp"),
        P("grp", "tp"),
        P("grp", "tp"),
        P("tp", "grp"),
    )
    return jax.shard_map(
        shards, mesh=mesh, in_specs=placed, out_specs=P(None, "tp", "grp"), check_vma=False
    )
```

```python
import jax
import jax.numpy as jnp
from jax import lax
from jax.experimental import pallas as pl
from jax.experimental.pallas import tpu as pltpu
from jax.sharding import PartitionSpec as P

D = 7168
SLOTS = 32
BLOCKS = 10
BLOCK = 64
HEADS = 16
KDIM = 576
RANK = 512
VH = 128
GRPS = 16
REQS = 256
POOL = 320
BATCH = 8
BATCHES = SLOTS // BATCH
PIECE = 10
PIECES = POOL // 2 // PIECE
RING = 3

score_scale = 192.0 ** (-0.5)
NT = (((1,), (1,)), ((), ()))
TN = (((0,), (0,)), ((), ()))

MESH = pl.DeviceIdType.MESH
WIDE = 512
COLS = 448
FFT = 2304
TAIL = 128
BF16 = jnp.bfloat16
F32 = jnp.float32


def layer_kernel(
    queries,
    fresh_hbm,
    cache,
    tables_hbm,
    lengths_hbm,
    rows_hbm,
    order_hbm,
    residual,
    gain_hbm,
    vup_hbm,
    wo_hbm,
    wg_hbm,
    wu_hbm,
    wd_hbm,
    out_ref,
    q_ref,
    fresh_ref,
    fresh_all,
    tables,
    lengths_ref,
    rows_ref,
    order_ref,
    gain_ref,
    vup,
    ring,
    values,
    scores,
    lat,
    lens,
    owner_row,
    owner,
    ring_sems,
    wo,
    wg,
    wu,
    wd,
    res,
    gathered,
    hiddens,
    select,
    stream,
    part,
    from_core,
    summed,
    from_x,
    normed,
    chunks_a,
    chunks_b,
    relay_a,
    relay_b,
    final_a,
    final_b,
    line_a,
    line_b,
    relay2_a,
    relay2_b,
    final2_a,
    final2_b,
    local_sems,
    send_sems,
    recv_sems,
):
    g, t = lax.axis_index("grp"), lax.axis_index("tp")
    y, z = g // 4, lax.rem(g, 4)
    x, core = t // 2, lax.rem(t, 2)

    def group_at(dy, dz):
        return lax.rem(y + dy + 4, 4) * 4 + lax.rem(z + dz + 4, 4)

    def tp_at(dx):
        return lax.rem(x + dx + 4, 4) * 2 + core

    partner = x * 2 + 1 - core
    used = []

    def remote(src, dst, device):
        i = len(used)
        copy = pltpu.make_async_remote_copy(
            src_ref=src,
            dst_ref=dst,
            send_sem=send_sems.at[i],
            recv_sem=recv_sems.at[i],
            device_id=device,
            device_id_type=MESH,
        )
        copy.start()
        used.append(copy)
        return copy

    local = []

    def bring(src, dst):
        copy = pltpu.make_async_copy(src, dst, local_sems.at[len(local)])
        copy.start()
        local.append(copy)
        return copy

    def piece(i):
        at = pl.ds(pl.multiple_of(i * PIECE * 128, PIECE * 128), PIECE * 128)
        at_ring = lax.rem(i, RING)
        return pltpu.make_async_copy(cache.at[:, at], ring.at[at_ring], ring_sems.at[at_ring])

    tables_in = bring(tables_hbm, tables)
    small = [
        bring(queries.at[0], q_ref.at[:, pl.ds(0, HEADS)]),
        bring(queries.at[1], q_ref.at[:, pl.ds(HEADS, HEADS)]),
        bring(fresh_hbm, fresh_ref),
        bring(lengths_hbm, lengths_ref),
        bring(rows_hbm, rows_ref),
        bring(order_hbm, order_ref),
        bring(gain_hbm, gain_ref),
    ]
    for i in range(RING):
        piece(i).start()

    barrier = pltpu.get_barrier_semaphore()
    greet = [(group_at(dy, dz), t) for dy, dz in ((1, 0), (-1, 0), (0, 1), (0, -1))]
    greet += [(g, tp_at(1)), (g, tp_at(-1)), (g, tp_at(2)), (g, partner)]
    for device in greet:
        pl.semaphore_signal(barrier, inc=1, device_id=device, device_id_type=MESH)
    pl.semaphore_wait(barrier, len(greet))

    def all_gather(bufs, cut):
        def slot(h, da, db):
            return group_at(da, db) if h == 0 else group_at(db, da)

        def send(h, da, db, to_a, to_b, half=None):
            at = slot(h, da, db)
            ref = bufs[h].at[at] if half is None else cut(bufs[h], at, half)
            return remote(ref, ref, (slot(h, to_a, to_b), t))

        along = [{}, {}]
        up, down, up2, down2 = [{}, {}], [{}, {}], [{}, {}], [{}, {}]

        def across(h, d):
            up[h][d] = send(h, d, 0, 0, 1)
            down[h][d] = send(h, d, 0, 0, -1)

        def pass_on(h, d):
            up[h][d].wait_recv()
            up2[h][d] = send(h, d, -1, 0, 1, 0)
            down[h][d].wait_recv()
            down2[h][d] = send(h, d, 1, 0, -1, 1)

        for h in range(2):
            along[h]["+"] = send(h, 0, 0, 1, 0)
            along[h]["-"] = send(h, 0, 0, -1, 0)
            across(h, 0)
        yield
        for h in range(2):
            along[h]["+"].wait_recv()
            along[h]["++"] = send(h, -1, 0, 1, 0, 0)
            across(h, -1)
            along[h]["-"].wait_recv()
            along[h]["--"] = send(h, 1, 0, -1, 0, 1)
            across(h, 1)
        for h in range(2):
            pass_on(h, 0)
        yield
        for h in range(2):
            along[h]["++"].wait_recv()
            along[h]["--"].wait_recv()
            across(h, 2)
        for d in (-1, 1):
            for h in range(2):
                pass_on(h, d)
        yield
        for h in range(2):
            pass_on(h, 2)
        yield
        for d in (0, -1, 1, 2):
            for h in range(2):
                up2[h][d].wait_recv()
                down2[h][d].wait_recv()

    def scatter_tp(turn):
        to_core = remote(part.at[turn, 1 - core], from_core.at[turn], (g, partner))
        to_core.wait_recv()
        for k in range(4):
            summed[turn, k] = (
                part[turn, core, k].astype(F32) + from_core[turn, k].astype(F32)
            ).astype(BF16)
        moves = []
        for i, dx in enumerate((1, -1, 2)):
            chip = lax.rem(x + dx + 4, 4)
            moves.append(remote(summed.at[turn, chip], from_x.at[turn, i], (g, tp_at(dx))))
        total = summed[turn, x].astype(F32)
        for i, move in enumerate(moves):
            move.wait_recv()
            total = total + from_x[turn, i].astype(F32)
        return total[:, :COLS]

    tables_in.wait()
    block_id = lax.broadcasted_iota(jnp.int32, (1, 384), 1)

    def own_blocks(slot, owners):
        for j in range(BLOCKS):
            owners = jnp.where(block_id == tables[j, slot], slot, owners)
        return owners

    owner_row[...] = lax.fori_loop(0, SLOTS, own_blocks, jnp.zeros((1, 384), jnp.int32), unroll=4)
    owner_in = bring(owner_row, owner)
    for copy in small:
        copy.wait()
    wo_in = bring(wo_hbm, wo)
    vup_in = bring(vup_hbm, vup)
    res_in = bring(residual, res)
    wg_in = bring(wg_hbm, wg)
    wu_in = bring(wu_hbm, wu)
    wd_in = bring(wd_hbm, wd)

    spread = lax.broadcasted_iota(jnp.int32, (GRPS, GRPS), 1)
    row_of = lax.broadcasted_iota(jnp.int32, (GRPS, GRPS), 0)
    ends = jnp.sum(jnp.where(spread <= row_of, rows_ref[...], 0), axis=1, keepdims=True)
    starts = jnp.sum(jnp.where(spread < row_of, rows_ref[...], 0), axis=1, keepdims=True)
    order = order_ref[...]
    in_group = jnp.logical_and(order >= starts, order < ends)
    group_id = lax.broadcasted_iota(jnp.int32, (GRPS, REQS), 0)
    spot = order - starts
    spot = (spot >> 3) * (GRPS * BATCH) + group_id * BATCH + (spot & 7)
    at = jnp.sum(jnp.where(in_group, spot, 0), axis=0, keepdims=True)
    matches = lax.broadcasted_iota(jnp.int32, (GRPS * SLOTS, REQS), 0) == at
    select[...] = jnp.where(matches, 1.0, 0.0).astype(BF16)
    group_row = lax.broadcasted_iota(jnp.int32, (1, GRPS), 1)
    my_start = jnp.sum(jnp.where(group_row < g, rows_ref[...], 0), axis=1, keepdims=True)
    my_live = jnp.sum(jnp.where(group_row == g, rows_ref[...], 0), axis=1, keepdims=True)
    slot_row = lax.broadcasted_iota(jnp.int32, (SLOTS, REQS), 0)
    named = jnp.logical_and(order - my_start == slot_row, slot_row < my_live)
    slot_len = jnp.sum(jnp.where(named, lengths_ref[...], 0), axis=1, keepdims=True)
    lens[...] = jnp.broadcast_to(slot_len, (SLOTS, 128))
    fresh_all[...] = fresh_ref[...].astype(F32)
    owner_in.wait()

    lane = lax.broadcasted_iota(jnp.int32, (2 * HEADS, 128), 1)

    def one_piece(i, carry):
        piece(i).wait()
        at_ring = lax.rem(i, RING)
        for c in range(PIECE):
            chunk = ring[at_ring, :, c * 128 : c * 128 + 128]
            which = i * PIECE + c
            both = [
                q_ref[owner[0, 2 * which + k]] for k in range(2)
            ]
            both = jnp.dot(
                jnp.concatenate(both, axis=0), chunk, preferred_element_type=F32
            )
            scores[which] = jnp.where(lane < BLOCK, both[: 2 * HEADS], both[2 * HEADS :])
            turned = chunk[:RANK, :].T
            values[2 * which] = turned[:BLOCK]
            values[2 * which + 1] = turned[BLOCK:]

        @pl.when(i + RING < PIECES)
        def _():
            piece(i + RING).start()

        return carry

    lax.fori_loop(0, PIECES, one_piece, 0)

    step_of = lax.broadcasted_iota(jnp.int32, (2 * HEADS, 1), 0) // HEADS
    PER = 4

    def some_slots(b, it):
        tiles, picks = [], []
        for k in range(PER):
            slot = b * BATCH + it * PER + k
            q = q_ref[slot].astype(F32)
            length = lens[pl.ds(slot, 1), :]
            mine, rows = [], []
            for j in range(BLOCKS // 2):
                one, two = tables[2 * j, slot], tables[2 * j + 1, slot]
                odd_one, odd_two = lax.rem(one, 2), lax.rem(two, 2)
                two_score = scores[lax.div(two, 2)]
                two_score = jnp.where(
                    lane * 0 + odd_one == odd_two, pltpu.roll(two_score, BLOCK, 1), two_score
                )
                position = lane + BLOCK * odd_one
                position = jnp.where(position < 2 * BLOCK, position, position - 2 * BLOCK)
                tile = jnp.where(position < BLOCK, scores[lax.div(one, 2)], two_score) * score_scale
                mine.append(jnp.where(position + 128 * j < length, tile, -jnp.inf))
                rows.append(values[one + (two - one) * odd_one])
                rows.append(values[two + (one - two) * odd_one])
            new = [fresh_all[n, pl.ds(slot, 1), :] for n in range(2)]
            now = jnp.sum(q * new[0], axis=1, keepdims=True) * score_scale
            later = jnp.sum(q * new[1], axis=1, keepdims=True) * score_scale
            later = jnp.where(step_of == 1, later, -jnp.inf)
            tiles.append((jnp.concatenate(mine, axis=1), now, later, new))
            picks.append(jnp.concatenate(rows, axis=0))
        for k in range(PER):
            tile, now, later, new = tiles[k]
            largest = jnp.maximum(jnp.max(tile, axis=1, keepdims=True), jnp.maximum(now, later))
            expo = jnp.exp(tile - largest)
            now = jnp.exp(now - largest)
            later = jnp.exp(later - largest)
            inverse = 1.0 / (jnp.sum(expo, axis=1, keepdims=True) + now + later)
            mixed = jnp.dot(expo.astype(BF16), picks[k], preferred_element_type=F32)
            mixed = mixed + now * new[0][:, :RANK] + later * new[1][:, :RANK]
            lat[it * PER + k] = mixed * inverse

    def cut_columns(ref, at, half):
        return ref.at[at, :, pl.ds(512 * half, 512)]

    running = []
    for b in range(BATCHES):

        def one_step(it, carry, b=b):
            some_slots(b, it)
            return carry

        lax.fori_loop(0, BATCH // PER, one_step, 0)
        if b == 0:
            vup_in.wait()
        for h in range(HEADS):
            both = jnp.concatenate([lat[:, h, :], lat[:, HEADS + h, :]], axis=0).astype(BF16)
            value = jnp.dot(both, vup[h], preferred_element_type=F32).astype(BF16)
            gathered[h // 8, b, g, :, (h % 8) * VH : (h % 8 + 1) * VH] = value
        running.append(all_gather([gathered.at[h, b] for h in range(2)], cut_columns))
        for one in running:
            next(one, None)

    wo_in.wait()
    part[:, :, :, :, 384:] = jnp.zeros(part.shape[:-1] + (128,), BF16)
    batch_rows = [[], []]
    for b in range(BATCHES):
        while next(running[b], True) is None:
            for one in running[b + 1 :]:
                next(one, None)
        both = [gathered[h, b].reshape(GRPS * 2 * BATCH, 1024) for h in range(2)]
        value = lax.dot_general(both[0], wo[:, :1024], NT, preferred_element_type=F32)
        value = value + lax.dot_general(both[1], wo[:, 1024:], NT, preferred_element_type=F32)
        value = value.reshape(GRPS, 2, BATCH, COLS)
        for s in range(2):
            batch_rows[s].append(value[:, s].reshape(GRPS * BATCH, COLS).astype(BF16))
    for s in range(2):
        value = jnp.concatenate(batch_rows[s], axis=0)
        placed = lax.dot_general(select[...], value, TN, preferred_element_type=F32).astype(BF16)
        for k in range(8):
            part[0, k % 2, k // 2, s * 32 : s * 32 + 32, :COLS] = placed[32 * k : 32 * k + 32]
    attention = scatter_tp(0)

    res_in.wait()
    mine = lax.broadcasted_iota(jnp.int32, (32, REQS), 1) == (
        lax.broadcasted_iota(jnp.int32, (32, REQS), 0) + t * 32
    )
    mine = jnp.where(mine, 1.0, 0.0).astype(BF16)
    for s in range(2):
        own = lax.dot_general(mine, res[s], NT, preferred_element_type=F32)
        stream[s * 32 : s * 32 + 32, :] = own + attention[s * 32 : s * 32 + 32]
    here = stream[...]
    squares = jnp.sum(here * here, axis=1, keepdims=True)
    high = squares.astype(BF16)
    low = (squares - high.astype(F32)).astype(BF16)
    lane = lax.broadcasted_iota(jnp.int32, (64, WIDE - COLS), 1)
    extra = jnp.where(lane == 0, high, jnp.where(lane == 1, low, jnp.zeros_like(high)))
    scaled = (here * gain_ref[...].astype(F32)).astype(BF16)
    scaled = jnp.concatenate([scaled, extra], axis=1)
    normed[2 * t] = scaled[:32]
    normed[2 * t + 1] = scaled[32:]

    def pair(index):
        return normed.at[pl.ds(2 * index, 2)]

    moves = [remote(pair(t), pair(t), (g, tp_at(dx))) for dx in (1, -1, 2)]
    moves.append(remote(pair(t), pair(t), (g, partner)))
    shares = []
    for move, dx in zip(moves[:3], (-1, 1, 2)):
        move.wait_recv()
        shares.append(remote(pair(tp_at(dx)), pair(tp_at(dx)), (g, partner)))
    for move in moves[3:] + shares:
        move.wait_recv()
    wg_in.wait()
    wu_in.wait()

    chunks, weight = (chunks_a, chunks_b), (wg, wu)
    relay, final, line = (relay_a, relay_b), (final_a, final_b), (line_a, line_b)
    relay2, final2 = (relay2_a, relay2_b), (final2_a, final2_b)
    cut = (1280, 1152)
    first = (pl.ds(0, 1280), pl.ds(0, 1152))
    second = (pl.ds(1280, 1152), pl.ds(1152, 1152))

    def along(h, d):
        return (group_at(d, 0) if h == 0 else group_at(0, d), t)

    def across(h, d):
        return along(1 - h, d)

    def product(h, i, d):
        blocks = []
        for k in range(4):
            b = lax.rem(y + d + 4, 4) * 4 + k if h == 0 else k * 4 + lax.rem(z + d + 4, 4)
            blocks.append(normed[b])
        rows = jnp.concatenate(blocks, axis=0)
        if h == 0:
            chunks[h][i, :, FFT:] = rows[:, 384:]
        rows = rows[:, :COLS]

        def one(n, carry):
            at = pl.ds(pl.multiple_of(n * 256, 256), 256)
            chunks[h][i, :, at] = jnp.dot(
                rows, weight[h][:, at], preferred_element_type=F32
            ).astype(BF16)
            return carry

        lax.fori_loop(0, FFT // 256, one, 0)

    def add(ref, index, part_cols, other):
        ref[index, :, part_cols] = (
            ref[index, :, part_cols].astype(F32) + other[...].astype(F32)
        ).astype(BF16)

    relays, finals = [None, None], [[], []]
    for h in range(2):
        product(h, 2, 2)
        relays[h] = (
            remote(chunks[h].at[2, :, first[h]], relay[h].at[0, :, first[h]], along(h, 1)),
            remote(chunks[h].at[2, :, second[h]], relay[h].at[1, :, pl.ds(0, 1152)], along(h, -1)),
        )
    for h in range(2):
        product(h, 1, 1)
        finals[h].append(
            remote(chunks[h].at[1, :, second[h]], final[h].at[0, :, second[h]], along(h, 1))
        )
        product(h, 3, -1)
        finals[h].append(
            remote(chunks[h].at[3, :, first[h]], final[h].at[1, :, first[h]], along(h, -1))
        )
    for h in range(2):
        relays[h][0].wait_recv()
        add(chunks[h], 1, first[h], relay[h].at[0, :, first[h]])
        finals[h].append(
            remote(chunks[h].at[1, :, first[h]], final[h].at[0, :, first[h]], along(h, 1))
        )
        relays[h][1].wait_recv()
        add(chunks[h], 3, second[h], relay[h].at[1, :, pl.ds(0, 1152)])
        finals[h].append(
            remote(chunks[h].at[3, :, second[h]], final[h].at[1, :, second[h]], along(h, -1))
        )
    for h in range(2):
        product(h, 0, 0)
    relays, finals2 = [None, None], [[], []]
    for h in range(2):
        for copy in finals[h]:
            copy.wait_recv()
        for k in range(4):
            at = pl.ds(32 * k, 32)
            line[h][k] = (
                chunks[h][0, at, :].astype(F32)
                + final[h][0, at, :].astype(F32)
                + final[h][1, at, :].astype(F32)
            ).astype(BF16)
        spot = z if h == 0 else y

        def place(d):
            return lax.rem(spot + d + 4, 4)

        far, ahead, behind = place(2), place(1), place(-1)
        relays[h] = (
            remote(line[h].at[far, :, first[h]], relay2[h].at[0, :, first[h]], across(h, 1)),
            remote(line[h].at[far, :, second[h]], relay2[h].at[1, :, pl.ds(0, 1152)], across(h, -1)),
        )
        finals2[h].append(
            remote(line[h].at[ahead, :, second[h]], final2[h].at[0, :, second[h]], across(h, 1))
        )
        finals2[h].append(
            remote(line[h].at[behind, :, first[h]], final2[h].at[1, :, first[h]], across(h, -1))
        )
    totals = []
    for h in range(2):
        spot = z if h == 0 else y
        ahead, behind = lax.rem(spot + 1, 4), lax.rem(spot + 3, 4)
        relays[h][0].wait_recv()
        add(line[h], ahead, first[h], relay2[h].at[0, :, first[h]])
        finals2[h].append(
            remote(line[h].at[ahead, :, first[h]], final2[h].at[0, :, first[h]], across(h, 1))
        )
        relays[h][1].wait_recv()
        add(line[h], behind, second[h], relay2[h].at[1, :, pl.ds(0, 1152)])
        finals2[h].append(
            remote(line[h].at[behind, :, second[h]], final2[h].at[1, :, second[h]], across(h, -1))
        )
    for h in range(2):
        for copy in finals2[h]:
            copy.wait_recv()
        spot = z if h == 0 else y
        totals.append(
            line[h][spot].astype(F32) + final2[h][0].astype(F32) + final2[h][1].astype(F32)
        )
    mean = (totals[0][:, FFT + 64 : FFT + 65] + totals[0][:, FFT + 65 : FFT + 66]) / D
    inverse_rms = lax.rsqrt(mean + 1e-06)
    gate = totals[0][:, :FFT] * inverse_rms
    up = totals[1] * inverse_rms
    hidden = (gate / (1.0 + jnp.exp(-gate)) * up).astype(BF16)
    for h in range(2):
        for k in range(2):
            hiddens[h, g, k] = hidden[16 * k : 16 * k + 16, 1152 * h : 1152 * h + 1152]
    for _ in all_gather([hiddens.at[0], hiddens.at[1]], lambda ref, at, half: ref.at[at, half]):
        pass

    wd_in.wait()
    for q in range(4):
        both = [hiddens[h, 4 * q : 4 * q + 4].reshape(128, 1152) for h in range(2)]
        value = lax.dot_general(both[0], wd[:, :1152], NT, preferred_element_type=F32)
        value = value + lax.dot_general(both[1], wd[:, 1152:], NT, preferred_element_type=F32)
        value = value.astype(BF16)
        for k in range(2):
            part[1, k, q, :, :COLS] = value[64 * k : 64 * k + 64]
    reduced = scatter_tp(1)
    for s in range(2):
        at = slice(32 * s, 32 * s + 32)
        out_ref[s] = (stream[at, :] + reduced[at]).astype(BF16)
    for copy in used:
        copy.wait_send()


def layer(
    queries,
    new_latent,
    latent_cache,
    tables,
    context_len,
    group_rows,
    request_order,
    residual,
    value_up,
    out_proj,
    norm_gain,
    gate_proj,
    up_proj,
    down_proj,
):
    hbm = pl.BlockSpec(memory_space=pl.ANY)
    copies = BATCHES * 40 + 40 + 4 + 4 + 7 + 12 + 12
    return pl.pallas_call(
        layer_kernel,
        out_shape=jax.ShapeDtypeStruct((2, 32, COLS), BF16),
        in_specs=[hbm] * 14,
        out_specs=pl.BlockSpec(memory_space=pltpu.VMEM),
        scratch_shapes=[
            pltpu.VMEM((SLOTS, 2 * HEADS, KDIM), BF16),
            pltpu.VMEM((2, SLOTS, KDIM), BF16),
            pltpu.VMEM((2, SLOTS, KDIM), F32),
            pltpu.SMEM((BLOCKS, SLOTS), jnp.int32),
            pltpu.VMEM((1, REQS), jnp.int32),
            pltpu.VMEM((1, GRPS), jnp.int32),
            pltpu.VMEM((1, REQS), jnp.int32),
            pltpu.VMEM((1, COLS), BF16),
            pltpu.VMEM((HEADS, RANK, VH), BF16),
            pltpu.VMEM((RING, KDIM, PIECE * 128), BF16),
            pltpu.VMEM((POOL, BLOCK, RANK), BF16),
            pltpu.VMEM((POOL // 2, 2 * HEADS, 128), F32),
            pltpu.VMEM((BATCH, 2 * HEADS, RANK), F32),
            pltpu.VMEM((SLOTS, 128), jnp.int32),
            pltpu.VMEM((1, 384), jnp.int32),
            pltpu.SMEM((1, 384), jnp.int32),
            pltpu.SemaphoreType.DMA((RING,)),
            pltpu.VMEM((COLS, 2048), BF16),
            pltpu.VMEM((COLS, FFT), BF16),
            pltpu.VMEM((COLS, FFT), BF16),
            pltpu.VMEM((COLS, FFT), BF16),
            pltpu.VMEM((2, COLS, REQS), BF16),
            pltpu.VMEM((2, BATCHES, GRPS, 2 * BATCH, 1024), BF16),
            pltpu.VMEM((2, GRPS, 2, 16, 1152), BF16),
            pltpu.VMEM((GRPS * SLOTS, REQS), BF16),
            pltpu.VMEM((64, COLS), F32),
            pltpu.VMEM((2, 2, 4, 64, WIDE), BF16),
            pltpu.VMEM((2, 4, 64, WIDE), BF16),
            pltpu.VMEM((2, 4, 64, WIDE), BF16),
            pltpu.VMEM((2, 3, 64, WIDE), BF16),
            pltpu.VMEM((16, 32, WIDE), BF16),
            pltpu.VMEM((4, 128, FFT + TAIL), BF16),
            pltpu.VMEM((4, 128, FFT), BF16),
            pltpu.VMEM((2, 128, 1280), BF16),
            pltpu.VMEM((2, 128, 1152), BF16),
            pltpu.VMEM((2, 128, FFT + TAIL), BF16),
            pltpu.VMEM((2, 128, FFT), BF16),
            pltpu.VMEM((4, 32, FFT + TAIL), BF16),
            pltpu.VMEM((4, 32, FFT), BF16),
            pltpu.VMEM((2, 32, 1280), BF16),
            pltpu.VMEM((2, 32, 1152), BF16),
            pltpu.VMEM((2, 32, FFT + TAIL), BF16),
            pltpu.VMEM((2, 32, FFT), BF16),
            pltpu.SemaphoreType.DMA((15,)),
            pltpu.SemaphoreType.DMA((copies,)),
            pltpu.SemaphoreType.DMA((copies,)),
        ],
        compiler_params=pltpu.CompilerParams(
            collective_id=0, has_side_effects=True, vmem_limit_bytes=63 << 20
        ),
    )(
        queries,
        new_latent,
        latent_cache.T,
        tables.T,
        context_len.reshape(1, REQS),
        group_rows.reshape(1, GRPS),
        request_order.reshape(1, REQS),
        jnp.swapaxes(residual, 1, 2),
        norm_gain.reshape(1, COLS),
        value_up,
        out_proj.T,
        gate_proj,
        up_proj,
        down_proj.T,
    )


def solution(mesh):
    placed = (
        P(None, "grp", "tp", None),
        P(None, "grp", None),
        P("grp", None),
        P("grp", None),
        P(),
        P(),
        P(),
        P(None, None, "grp"),
        P("tp", None, None),
        P("tp", "grp"),
        P("grp"),
        P("grp", "tp"),
        P("grp", "tp"),
        P("tp", "grp"),
    )
    return jax.shard_map(
        layer, mesh=mesh, in_specs=placed, out_specs=P(None, "tp", "grp"), check_vma=False
    )
```

```python
import jax
import jax.numpy as jnp
from jax import lax
from jax.experimental import pallas as pl
from jax.experimental.pallas import tpu as pltpu
from jax.sharding import PartitionSpec as P

D = 7168
SLOTS = 32
BLOCKS = 10
BLOCK = 64
HEADS = 16
KDIM = 576
RANK = 512
VH = 128
GRPS = 16
REQS = 256
POOL = 320
BATCH = 16
BATCHES = SLOTS // BATCH
PIECE = 10
PIECES = POOL // 2 // PIECE
RING = 3

score_scale = 192.0 ** (-0.5)
NT = (((1,), (1,)), ((), ()))
TN = (((0,), (0,)), ((), ()))

MESH = pl.DeviceIdType.MESH
WIDE = 512
COLS = 448
FFT = 2304
TAIL = 128
BF16 = jnp.bfloat16
F32 = jnp.float32


def layer_kernel(
    queries,
    fresh_hbm,
    cache,
    tables_hbm,
    lengths_hbm,
    rows_hbm,
    order_hbm,
    residual,
    gain_hbm,
    vup_hbm,
    wo_hbm,
    wg_hbm,
    wu_hbm,
    wd_hbm,
    out_ref,
    q_ref,
    fresh_ref,
    fresh_all,
    tables,
    lengths_ref,
    rows_ref,
    order_ref,
    gain_ref,
    vup,
    ring,
    values,
    scores,
    lat,
    lens,
    owner_row,
    owner,
    ring_sems,
    wo,
    wg,
    wu,
    wd,
    res,
    gathered,
    hiddens,
    select,
    stream,
    part,
    from_core,
    summed,
    from_x,
    normed,
    chunks_a,
    chunks_b,
    relay_a,
    relay_b,
    final_a,
    final_b,
    line_a,
    line_b,
    relay2_a,
    relay2_b,
    final2_a,
    final2_b,
    local_sems,
    send_sems,
    recv_sems,
):
    g, t = lax.axis_index("grp"), lax.axis_index("tp")
    y, z = g // 4, lax.rem(g, 4)
    x, core = t // 2, lax.rem(t, 2)

    def group_at(dy, dz):
        return lax.rem(y + dy + 4, 4) * 4 + lax.rem(z + dz + 4, 4)

    def tp_at(dx):
        return lax.rem(x + dx + 4, 4) * 2 + core

    partner = x * 2 + 1 - core
    used = []

    def remote(src, dst, device):
        i = len(used)
        copy = pltpu.make_async_remote_copy(
            src_ref=src,
            dst_ref=dst,
            send_sem=send_sems.at[i],
            recv_sem=recv_sems.at[i],
            device_id=device,
            device_id_type=MESH,
        )
        copy.start()
        used.append(copy)
        return copy

    local = []

    def bring(src, dst):
        copy = pltpu.make_async_copy(src, dst, local_sems.at[len(local)])
        copy.start()
        local.append(copy)
        return copy

    def piece(i):
        at = pl.ds(pl.multiple_of(i * PIECE * 128, PIECE * 128), PIECE * 128)
        at_ring = lax.rem(i, RING)
        return pltpu.make_async_copy(cache.at[:, at], ring.at[at_ring], ring_sems.at[at_ring])

    tables_in = bring(tables_hbm, tables)
    small = [
        bring(queries.at[0], q_ref.at[:, pl.ds(0, HEADS)]),
        bring(queries.at[1], q_ref.at[:, pl.ds(HEADS, HEADS)]),
        bring(fresh_hbm, fresh_ref),
        bring(lengths_hbm, lengths_ref),
        bring(rows_hbm, rows_ref),
        bring(order_hbm, order_ref),
        bring(gain_hbm, gain_ref),
    ]
    for i in range(RING):
        piece(i).start()

    barrier = pltpu.get_barrier_semaphore()
    greet = [(group_at(dy, dz), t) for dy, dz in ((1, 0), (-1, 0), (0, 1), (0, -1))]
    greet += [(g, tp_at(1)), (g, tp_at(-1)), (g, tp_at(2)), (g, partner)]
    for device in greet:
        pl.semaphore_signal(barrier, inc=1, device_id=device, device_id_type=MESH)
    pl.semaphore_wait(barrier, len(greet))

    def all_gather(bufs, cut):
        def slot(h, da, db):
            return group_at(da, db) if h == 0 else group_at(db, da)

        def send(h, da, db, to_a, to_b, half=None):
            at = slot(h, da, db)
            ref = bufs[h].at[at] if half is None else cut(bufs[h], at, half)
            return remote(ref, ref, (slot(h, to_a, to_b), t))

        along = [{}, {}]
        up, down, up2, down2 = [{}, {}], [{}, {}], [{}, {}], [{}, {}]

        def across(h, d):
            up[h][d] = send(h, d, 0, 0, 1)
            down[h][d] = send(h, d, 0, 0, -1)

        def pass_on(h, d):
            up[h][d].wait_recv()
            up2[h][d] = send(h, d, -1, 0, 1, 0)
            down[h][d].wait_recv()
            down2[h][d] = send(h, d, 1, 0, -1, 1)

        for h in range(2):
            along[h]["+"] = send(h, 0, 0, 1, 0)
            along[h]["-"] = send(h, 0, 0, -1, 0)
            across(h, 0)
        yield
        for h in range(2):
            along[h]["+"].wait_recv()
            along[h]["++"] = send(h, -1, 0, 1, 0, 0)
            across(h, -1)
            along[h]["-"].wait_recv()
            along[h]["--"] = send(h, 1, 0, -1, 0, 1)
            across(h, 1)
        for h in range(2):
            pass_on(h, 0)
        yield
        for h in range(2):
            along[h]["++"].wait_recv()
            along[h]["--"].wait_recv()
            across(h, 2)
        for d in (-1, 1):
            for h in range(2):
                pass_on(h, d)
        yield
        for h in range(2):
            pass_on(h, 2)
        yield
        for d in (0, -1, 1, 2):
            for h in range(2):
                up2[h][d].wait_recv()
                down2[h][d].wait_recv()

    def scatter_tp(turn, s):
        to_core = remote(part.at[turn, s, 1 - core], from_core.at[turn, s], (g, partner))
        yield
        to_core.wait_recv()
        for k in range(4):
            summed[turn, s, k] = (
                part[turn, s, core, k].astype(F32) + from_core[turn, s, k].astype(F32)
            ).astype(BF16)
        moves = []
        for i, dx in enumerate((1, -1, 2)):
            chip = lax.rem(x + dx + 4, 4)
            moves.append(
                remote(summed.at[turn, s, chip], from_x.at[turn, s, i], (g, tp_at(dx)))
            )
        yield
        total = summed[turn, s, x].astype(F32)
        for i, move in enumerate(moves):
            move.wait_recv()
            total = total + from_x[turn, s, i].astype(F32)
        return total[:, :COLS]

    tables_in.wait()
    block_id = lax.broadcasted_iota(jnp.int32, (1, 384), 1)

    def own_blocks(slot, owners):
        for j in range(BLOCKS):
            owners = jnp.where(block_id == tables[j, slot], slot, owners)
        return owners

    owner_row[...] = lax.fori_loop(0, SLOTS, own_blocks, jnp.zeros((1, 384), jnp.int32), unroll=4)
    owner_in = bring(owner_row, owner)
    for copy in small:
        copy.wait()
    spread = lax.broadcasted_iota(jnp.int32, (GRPS, GRPS), 1)
    row_of = lax.broadcasted_iota(jnp.int32, (GRPS, GRPS), 0)
    ends = jnp.sum(jnp.where(spread <= row_of, rows_ref[...], 0), axis=1, keepdims=True)
    starts = jnp.sum(jnp.where(spread < row_of, rows_ref[...], 0), axis=1, keepdims=True)
    order = order_ref[...]
    in_group = jnp.logical_and(order >= starts, order < ends)
    group_id = lax.broadcasted_iota(jnp.int32, (GRPS, REQS), 0)
    spot = order - starts
    spot = (spot >> 4) * (GRPS * BATCH) + group_id * BATCH + (spot & 15)
    at = jnp.sum(jnp.where(in_group, spot, 0), axis=0, keepdims=True)
    matches = lax.broadcasted_iota(jnp.int32, (GRPS * SLOTS, REQS), 0) == at
    select[...] = jnp.where(matches, 1.0, 0.0).astype(BF16)
    group_row = lax.broadcasted_iota(jnp.int32, (1, GRPS), 1)
    my_start = jnp.sum(jnp.where(group_row < g, rows_ref[...], 0), axis=1, keepdims=True)
    my_live = jnp.sum(jnp.where(group_row == g, rows_ref[...], 0), axis=1, keepdims=True)
    slot_row = lax.broadcasted_iota(jnp.int32, (SLOTS, REQS), 0)
    named = jnp.logical_and(order - my_start == slot_row, slot_row < my_live)
    slot_len = jnp.sum(jnp.where(named, lengths_ref[...], 0), axis=1, keepdims=True)
    lens[...] = jnp.broadcast_to(slot_len, (SLOTS, 128))
    fresh_all[...] = fresh_ref[...].astype(F32)
    owner_in.wait()

    lane = lax.broadcasted_iota(jnp.int32, (2 * HEADS, 128), 1)

    def one_piece(i, carry):
        piece(i).wait()
        at_ring = lax.rem(i, RING)
        for c in range(PIECE):
            chunk = ring[at_ring, :, c * 128 : c * 128 + 128]
            which = i * PIECE + c
            both = [
                q_ref[owner[0, 2 * which + k]] for k in range(2)
            ]
            both = jnp.dot(
                jnp.concatenate(both, axis=0), chunk, preferred_element_type=F32
            )
            scores[which] = jnp.where(lane < BLOCK, both[: 2 * HEADS], both[2 * HEADS :])
            turned = chunk[:RANK, :].T
            values[2 * which] = turned[:BLOCK]
            values[2 * which + 1] = turned[BLOCK:]

        @pl.when(i + RING < PIECES)
        def _():
            piece(i + RING).start()

        return carry

    lax.fori_loop(0, PIECES, one_piece, 0)
    vup_in = bring(vup_hbm, vup)
    wo_in = bring(wo_hbm, wo)
    res_in = bring(residual, res)
    wg_in = bring(wg_hbm, wg)
    wu_in = bring(wu_hbm, wu)
    wd_in = bring(wd_hbm, wd)

    step_of = lax.broadcasted_iota(jnp.int32, (2 * HEADS, 1), 0) // HEADS
    PER = 4

    def some_slots(b, it):
        tiles, picks = [], []
        for k in range(PER):
            slot = b * BATCH + it * PER + k
            q = q_ref[slot].astype(F32)
            length = lens[pl.ds(slot, 1), :]
            mine, rows = [], []
            for j in range(BLOCKS // 2):
                one, two = tables[2 * j, slot], tables[2 * j + 1, slot]
                odd_one, odd_two = lax.rem(one, 2), lax.rem(two, 2)
                two_score = scores[lax.div(two, 2)]
                two_score = jnp.where(
                    lane * 0 + odd_one == odd_two, pltpu.roll(two_score, BLOCK, 1), two_score
                )
                position = lane + BLOCK * odd_one
                position = jnp.where(position < 2 * BLOCK, position, position - 2 * BLOCK)
                tile = jnp.where(position < BLOCK, scores[lax.div(one, 2)], two_score) * score_scale
                mine.append(jnp.where(position + 128 * j < length, tile, -jnp.inf))
                rows.append(values[one + (two - one) * odd_one])
                rows.append(values[two + (one - two) * odd_one])
            new = [fresh_all[n, pl.ds(slot, 1), :] for n in range(2)]
            now = jnp.sum(q * new[0], axis=1, keepdims=True) * score_scale
            later = jnp.sum(q * new[1], axis=1, keepdims=True) * score_scale
            later = jnp.where(step_of == 1, later, -jnp.inf)
            tiles.append((jnp.concatenate(mine, axis=1), now, later, new))
            picks.append(jnp.concatenate(rows, axis=0))
        for k in range(PER):
            tile, now, later, new = tiles[k]
            largest = jnp.maximum(jnp.max(tile, axis=1, keepdims=True), jnp.maximum(now, later))
            expo = jnp.exp(tile - largest)
            now = jnp.exp(now - largest)
            later = jnp.exp(later - largest)
            inverse = 1.0 / (jnp.sum(expo, axis=1, keepdims=True) + now + later)
            mixed = jnp.dot(expo.astype(BF16), picks[k], preferred_element_type=F32)
            mixed = mixed + now * new[0][:, :RANK] + later * new[1][:, :RANK]
            lat[it * PER + k] = mixed * inverse

    def cut_heads(ref, at, half):
        return ref.at[at, :, pl.ds(512 * half, 512)]

    def cut_hidden(ref, at, half):
        return ref.at[at, :, pl.ds(0, 640) if half == 0 else pl.ds(640, 512)]

    part[:, :, :, :, :, 384:] = jnp.zeros(part.shape[:-1] + (128,), BF16)
    first = (pl.ds(0, 1280), pl.ds(0, 1152))
    second = (pl.ds(1280, 1152), pl.ds(1152, 1152))
    rest = pl.ds(0, 1152)
    chunks, weight = (chunks_a, chunks_b), (wg, wu)
    relay, final, line = (relay_a, relay_b), (final_a, final_b), (line_a, line_b)
    relay2, final2 = (relay2_a, relay2_b), (final2_a, final2_b)

    def along(h, d):
        return (group_at(d, 0) if h == 0 else group_at(0, d), t)

    def across(h, d):
        return along(1 - h, d)

    def product(s, h):
        blocks = []
        for d in range(4):
            for k in range(4):
                b = lax.rem(y + d, 4) * 4 + k if h == 0 else k * 4 + lax.rem(z + d, 4)
                blocks.append(normed[s, b])
        rows = jnp.concatenate(blocks, axis=0)
        if h == 0:
            for d in range(4):
                chunks[h][s, d, :, FFT:] = rows[64 * d : 64 * d + 64, 384:]
        rows = rows[:, :COLS]
        for n in range(3):
            at = slice(768 * n, 768 * n + 768)
            value = jnp.dot(rows, weight[h][:, at], preferred_element_type=F32).astype(BF16)
            for d in range(4):
                chunks[h][s, d, :, at] = value[64 * d : 64 * d + 64]

    def add(ref, s, index, columns, other):
        ref[s, index, :, columns] = (
            ref[s, index, :, columns].astype(F32) + other[...].astype(F32)
        ).astype(BF16)

    def after_heads(s):
        if s == 0:
            wo_in.wait()
        rows = []
        for b in range(BATCHES):
            both = [gathered[h, s, b].reshape(GRPS * BATCH, 1024) for h in range(2)]
            value = lax.dot_general(both[0], wo[:, :1024], NT, preferred_element_type=F32)
            value = value + lax.dot_general(both[1], wo[:, 1024:], NT, preferred_element_type=F32)
            rows.append(value.astype(BF16))
        value = jnp.concatenate(rows, axis=0)
        placed = lax.dot_general(select[...], value, TN, preferred_element_type=F32).astype(BF16)
        for k in range(8):
            part[0, s, k % 2, k // 2, :, :COLS] = placed[32 * k : 32 * k + 32]
        attention = yield from scatter_tp(0, s)

        if s == 0:
            res_in.wait()
        mine = lax.broadcasted_iota(jnp.int32, (32, REQS), 1) == (
            lax.broadcasted_iota(jnp.int32, (32, REQS), 0) + t * 32
        )
        mine = jnp.where(mine, 1.0, 0.0).astype(BF16)
        here = lax.dot_general(mine, res[s], NT, preferred_element_type=F32) + attention
        stream[s] = here
        squares = jnp.sum(here * here, axis=1, keepdims=True)
        high = squares.astype(BF16)
        low = (squares - high.astype(F32)).astype(BF16)
        extra_lane = lax.broadcasted_iota(jnp.int32, (32, WIDE - COLS), 1)
        extra = jnp.where(
            extra_lane == 0, high, jnp.where(extra_lane == 1, low, jnp.zeros_like(high))
        )
        scaled = (here * gain_ref[...].astype(F32)).astype(BF16)
        scaled = jnp.concatenate([scaled, extra], axis=1)
        normed[s, 2 * t] = scaled[:16]
        normed[s, 2 * t + 1] = scaled[16:]

        def pair(index):
            return normed.at[s, pl.ds(2 * index, 2)]

        moves = [remote(pair(t), pair(t), (g, tp_at(dx))) for dx in (1, -1, 2)]
        moves.append(remote(pair(t), pair(t), (g, partner)))
        yield
        shares = []
        for move, dx in zip(moves[:3], (-1, 1, 2)):
            move.wait_recv()
            shares.append(remote(pair(tp_at(dx)), pair(tp_at(dx)), (g, partner)))
        yield
        for move in moves[3:] + shares:
            move.wait_recv()
        if s == 0:
            wg_in.wait()
            wu_in.wait()

        relays, finals, finals2 = [None, None], [[], []], [[], []]
        for h in range(2):
            product(s, h)
            relays[h] = (
                remote(
                    chunks[h].at[s, 2, :, first[h]], relay[h].at[s, 0, :, first[h]], along(h, 1)
                ),
                remote(chunks[h].at[s, 2, :, second[h]], relay[h].at[s, 1, :, rest], along(h, -1)),
            )
            finals[h].append(
                remote(
                    chunks[h].at[s, 1, :, second[h]], final[h].at[s, 0, :, second[h]], along(h, 1)
                )
            )
            finals[h].append(
                remote(
                    chunks[h].at[s, 3, :, first[h]], final[h].at[s, 1, :, first[h]], along(h, -1)
                )
            )
        yield
        for h in range(2):
            relays[h][0].wait_recv()
            add(chunks[h], s, 1, first[h], relay[h].at[s, 0, :, first[h]])
            finals[h].append(
                remote(
                    chunks[h].at[s, 1, :, first[h]], final[h].at[s, 0, :, first[h]], along(h, 1)
                )
            )
            relays[h][1].wait_recv()
            add(chunks[h], s, 3, second[h], relay[h].at[s, 1, :, rest])
            finals[h].append(
                remote(
                    chunks[h].at[s, 3, :, second[h]], final[h].at[s, 1, :, second[h]], along(h, -1)
                )
            )
        yield
        for h in range(2):
            for copy in finals[h]:
                copy.wait_recv()
            for k in range(4):
                at = pl.ds(16 * k, 16)
                line[h][s, k] = (
                    chunks[h][s, 0, at, :].astype(F32)
                    + final[h][s, 0, at, :].astype(F32)
                    + final[h][s, 1, at, :].astype(F32)
                ).astype(BF16)
            place = z if h == 0 else y
            far, ahead, behind = [lax.rem(place + d, 4) for d in (2, 1, 3)]
            relays[h] = (
                remote(
                    line[h].at[s, far, :, first[h]], relay2[h].at[s, 0, :, first[h]], across(h, 1)
                ),
                remote(
                    line[h].at[s, far, :, second[h]], relay2[h].at[s, 1, :, rest], across(h, -1)
                ),
            )
            finals2[h].append(
                remote(
                    line[h].at[s, ahead, :, second[h]],
                    final2[h].at[s, 0, :, second[h]],
                    across(h, 1),
                )
            )
            finals2[h].append(
                remote(
                    line[h].at[s, behind, :, first[h]],
                    final2[h].at[s, 1, :, first[h]],
                    across(h, -1),
                )
            )
        yield
        for h in range(2):
            place = z if h == 0 else y
            ahead, behind = lax.rem(place + 1, 4), lax.rem(place + 3, 4)
            relays[h][0].wait_recv()
            add(line[h], s, ahead, first[h], relay2[h].at[s, 0, :, first[h]])
            finals2[h].append(
                remote(
                    line[h].at[s, ahead, :, first[h]],
                    final2[h].at[s, 0, :, first[h]],
                    across(h, 1),
                )
            )
            relays[h][1].wait_recv()
            add(line[h], s, behind, second[h], relay2[h].at[s, 1, :, rest])
            finals2[h].append(
                remote(
                    line[h].at[s, behind, :, second[h]],
                    final2[h].at[s, 1, :, second[h]],
                    across(h, -1),
                )
            )
        yield
        totals = []
        for h in range(2):
            for copy in finals2[h]:
                copy.wait_recv()
            place = z if h == 0 else y
            totals.append(
                line[h][s, place].astype(F32)
                + final2[h][s, 0].astype(F32)
                + final2[h][s, 1].astype(F32)
            )
        mean = (totals[0][:, FFT + 64 : FFT + 65] + totals[0][:, FFT + 65 : FFT + 66]) / D
        inverse_rms = lax.rsqrt(mean + 1e-06)
        gate = totals[0][:, :FFT] * inverse_rms
        up = totals[1] * inverse_rms
        hidden = (gate / (1.0 + jnp.exp(-gate)) * up).astype(BF16)
        for h in range(2):
            hiddens[h, s, g] = hidden[:, 1152 * h : 1152 * h + 1152]
        yield from all_gather([hiddens.at[h, s] for h in range(2)], cut_hidden)

        if s == 0:
            wd_in.wait()
        both = [hiddens[h, s].reshape(REQS, 1152) for h in range(2)]
        value = lax.dot_general(both[0], wd[:, :1152], NT, preferred_element_type=F32)
        value = value + lax.dot_general(both[1], wd[:, 1152:], NT, preferred_element_type=F32)
        value = value.astype(BF16)
        for k in range(8):
            part[1, s, k % 2, k // 2, :, :COLS] = value[32 * k : 32 * k + 32]
        reduced = yield from scatter_tp(1, s)
        out_ref[s] = (stream[s] + reduced).astype(BF16)

    def slots(b, low, high):
        def one_step(it, carry):
            some_slots(b, it)
            return carry

        lax.fori_loop(low, high, one_step, 0)

    def raise_values(b):
        for h in range(HEADS):
            both = jnp.concatenate([lat[:, h, :], lat[:, HEADS + h, :]], axis=0).astype(BF16)
            value = jnp.dot(both, vup[h], preferred_element_type=F32).astype(BF16)
            for s in range(2):
                gathered[h // 8, s, b, g, :, (h % 8) * VH : (h % 8 + 1) * VH] = value[
                    BATCH * s : BATCH * s + BATCH
                ]

    heads = [
        [all_gather([gathered.at[h, s, b] for h in range(2)], cut_heads) for b in range(2)]
        for s in range(2)
    ]
    late = [after_heads(s) for s in range(2)]

    def go(*turns):
        for one in turns:
            next(one, None)

    slots(0, 0, 4)
    vup_in.wait()
    raise_values(0)
    go(heads[0][0])
    slots(1, 0, 2)
    go(heads[0][0])
    slots(1, 2, 4)
    raise_values(1)
    go(heads[0][1], heads[0][0])
    go(heads[1][0], heads[0][1], heads[0][0])
    go(heads[0][1], heads[0][0], heads[1][1])
    go(heads[0][1], heads[1][0], heads[0][1])
    go(late[0], heads[1][0], heads[1][1])
    go(late[0], heads[1][0], heads[1][1])
    go(late[0], heads[1][0], heads[1][1])
    go(late[0], late[0], heads[1][1])
    go(late[1], late[0], late[1], late[1], late[1], late[1])
    for _ in range(9):
        go(late[0], late[1])
    go(late[1])
    for copy in used:
        copy.wait_send()


def layer(
    queries,
    new_latent,
    latent_cache,
    tables,
    context_len,
    group_rows,
    request_order,
    residual,
    value_up,
    out_proj,
    norm_gain,
    gate_proj,
    up_proj,
    down_proj,
):
    hbm = pl.BlockSpec(memory_space=pl.ANY)
    copies = 4 * 40 + 2 * 40 + 4 * 4 + 2 * 7 + 2 * 24
    return pl.pallas_call(
        layer_kernel,
        out_shape=jax.ShapeDtypeStruct((2, 32, COLS), BF16),
        in_specs=[hbm] * 14,
        out_specs=pl.BlockSpec(memory_space=pltpu.VMEM),
        scratch_shapes=[
            pltpu.VMEM((SLOTS, 2 * HEADS, KDIM), BF16),
            pltpu.VMEM((2, SLOTS, KDIM), BF16),
            pltpu.VMEM((2, SLOTS, KDIM), F32),
            pltpu.SMEM((BLOCKS, SLOTS), jnp.int32),
            pltpu.VMEM((1, REQS), jnp.int32),
            pltpu.VMEM((1, GRPS), jnp.int32),
            pltpu.VMEM((1, REQS), jnp.int32),
            pltpu.VMEM((1, COLS), BF16),
            pltpu.VMEM((HEADS, RANK, VH), BF16),
            pltpu.VMEM((RING, KDIM, PIECE * 128), BF16),
            pltpu.VMEM((POOL, BLOCK, RANK), BF16),
            pltpu.VMEM((POOL // 2, 2 * HEADS, 128), F32),
            pltpu.VMEM((BATCH, 2 * HEADS, RANK), F32),
            pltpu.VMEM((SLOTS, 128), jnp.int32),
            pltpu.VMEM((1, 384), jnp.int32),
            pltpu.SMEM((1, 384), jnp.int32),
            pltpu.SemaphoreType.DMA((RING,)),
            pltpu.VMEM((COLS, 2048), BF16),
            pltpu.VMEM((COLS, FFT), BF16),
            pltpu.VMEM((COLS, FFT), BF16),
            pltpu.VMEM((COLS, FFT), BF16),
            pltpu.VMEM((2, COLS, REQS), BF16),
            pltpu.VMEM((2, 2, BATCHES, GRPS, BATCH, 1024), BF16),
            pltpu.VMEM((2, 2, GRPS, 16, 1152), BF16),
            pltpu.VMEM((GRPS * SLOTS, REQS), BF16),
            pltpu.VMEM((2, 32, COLS), F32),
            pltpu.VMEM((2, 2, 2, 4, 32, WIDE), BF16),
            pltpu.VMEM((2, 2, 4, 32, WIDE), BF16),
            pltpu.VMEM((2, 2, 4, 32, WIDE), BF16),
            pltpu.VMEM((2, 2, 3, 32, WIDE), BF16),
            pltpu.VMEM((2, 16, 16, WIDE), BF16),
            pltpu.VMEM((2, 4, 64, FFT + TAIL), BF16),
            pltpu.VMEM((2, 4, 64, FFT), BF16),
            pltpu.VMEM((2, 2, 64, 1280), BF16),
            pltpu.VMEM((2, 2, 64, 1152), BF16),
            pltpu.VMEM((2, 2, 64, FFT + TAIL), BF16),
            pltpu.VMEM((2, 2, 64, FFT), BF16),
            pltpu.VMEM((2, 4, 16, FFT + TAIL), BF16),
            pltpu.VMEM((2, 4, 16, FFT), BF16),
            pltpu.VMEM((2, 2, 16, 1280), BF16),
            pltpu.VMEM((2, 2, 16, 1152), BF16),
            pltpu.VMEM((2, 2, 16, FFT + TAIL), BF16),
            pltpu.VMEM((2, 2, 16, FFT), BF16),
            pltpu.SemaphoreType.DMA((15,)),
            pltpu.SemaphoreType.DMA((copies,)),
            pltpu.SemaphoreType.DMA((copies,)),
        ],
        compiler_params=pltpu.CompilerParams(
            collective_id=0, has_side_effects=True, vmem_limit_bytes=63 << 20
        ),
    )(
        queries,
        new_latent,
        latent_cache.T,
        tables.T,
        context_len.reshape(1, REQS),
        group_rows.reshape(1, GRPS),
        request_order.reshape(1, REQS),
        jnp.swapaxes(residual, 1, 2),
        norm_gain.reshape(1, COLS),
        value_up,
        out_proj.T,
        gate_proj,
        up_proj,
        down_proj.T,
    )


def solution(mesh):
    placed = (
        P(None, "grp", "tp", None),
        P(None, "grp", None),
        P("grp", None),
        P("grp", None),
        P(),
        P(),
        P(),
        P(None, None, "grp"),
        P("tp", None, None),
        P("tp", "grp"),
        P("grp"),
        P("grp", "tp"),
        P("grp", "tp"),
        P("tp", "grp"),
    )
    return jax.shard_map(
        layer, mesh=mesh, in_specs=placed, out_specs=P(None, "tp", "grp"), check_vma=False
    )
```

```python
import jax
import jax.numpy as jnp
from jax import lax
from jax.experimental import pallas as pl
from jax.experimental.pallas import tpu as pltpu
from jax.sharding import PartitionSpec as P

D = 7168
SLOTS = 32
BLOCKS = 10
BLOCK = 64
HEADS = 16
KDIM = 576
RANK = 512
VH = 128
GRPS = 16
REQS = 256
POOL = 320
BATCH = 16
BATCHES = SLOTS // BATCH
PIECE = 10
PIECES = POOL // 2 // PIECE
RING = 4

score_scale = 192.0 ** (-0.5)
NT = (((1,), (1,)), ((), ()))
TN = (((0,), (0,)), ((), ()))

MESH = pl.DeviceIdType.MESH
WIDE = 512
COLS = 448
FFT = 2304
TAIL = 128
BF16 = jnp.bfloat16
F32 = jnp.float32


def layer_kernel(
    queries,
    fresh_hbm,
    cache,
    tables_hbm,
    lengths_hbm,
    rows_hbm,
    order_hbm,
    residual,
    gain_hbm,
    vup_hbm,
    wo_hbm,
    wg_hbm,
    wu_hbm,
    wd_hbm,
    out_ref,
    q_ref,
    fresh_ref,
    fresh_all,
    tables,
    lengths_ref,
    rows_ref,
    order_ref,
    gain_ref,
    vup,
    ring,
    values,
    scores,
    lat,
    lens,
    owner_row,
    owner,
    ring_sems,
    wg,
    wu,
    res,
    gathered,
    hiddens,
    select,
    stream,
    part,
    from_core,
    from_x,
    normed,
    chunks_a,
    chunks_b,
    relay_a,
    relay_b,
    final_a,
    final_b,
    line_a,
    line_b,
    final2_a,
    final2_b,
    local_sems,
    send_sems,
    recv_sems,
):
    g, t = lax.axis_index("grp"), lax.axis_index("tp")
    y, z = g // 4, lax.rem(g, 4)
    x, core = t // 2, lax.rem(t, 2)

    def group_at(dy, dz):
        return lax.rem(y + dy + 4, 4) * 4 + lax.rem(z + dz + 4, 4)

    def tp_at(dx):
        return lax.rem(x + dx + 4, 4) * 2 + core

    partner = x * 2 + 1 - core
    used = []

    def remote(src, dst, device):
        i = len(used)
        copy = pltpu.make_async_remote_copy(
            src_ref=src,
            dst_ref=dst,
            send_sem=send_sems.at[i],
            recv_sem=recv_sems.at[i],
            device_id=device,
            device_id_type=MESH,
        )
        copy.start()
        used.append(copy)
        return copy

    local = []

    def bring(src, dst):
        copy = pltpu.make_async_copy(src, dst, local_sems.at[len(local)])
        copy.start()
        local.append(copy)
        return copy

    def piece(i):
        at = pl.ds(pl.multiple_of(i * PIECE * 128, PIECE * 128), PIECE * 128)
        at_ring = lax.rem(i, RING)
        return pltpu.make_async_copy(cache.at[:, at], ring.at[at_ring], ring_sems.at[at_ring])

    tables_in = bring(tables_hbm, tables)
    queries_in = [
        bring(queries.at[0], q_ref.at[:, pl.ds(0, HEADS)]),
        bring(queries.at[1], q_ref.at[:, pl.ds(HEADS, HEADS)]),
    ]
    for i in range(RING):
        piece(i).start()
    small = [
        bring(fresh_hbm, fresh_ref),
        bring(lengths_hbm, lengths_ref),
        bring(rows_hbm, rows_ref),
        bring(order_hbm, order_ref),
        bring(gain_hbm, gain_ref),
    ]

    barrier = pltpu.get_barrier_semaphore()
    greet = [(group_at(dy, dz), t) for dy, dz in ((1, 0), (-1, 0), (2, 0), (0, 1), (0, -1), (0, 2))]
    greet += [(g, tp_at(1)), (g, tp_at(-1)), (g, tp_at(2)), (g, partner)]
    for device in greet:
        pl.semaphore_signal(barrier, inc=1, device_id=device, device_id_type=MESH)

    def all_gather(bufs, cut):
        def slot(h, da, db):
            return group_at(da, db) if h == 0 else group_at(db, da)

        def send(h, da, db, to_a, to_b, half=None):
            at = slot(h, da, db)
            ref = bufs[h].at[at] if half is None else cut(bufs[h], at, half)
            return remote(ref, ref, (slot(h, to_a, to_b), t))

        along = [{}, {}]
        up, down, up2, down2 = [{}, {}], [{}, {}], [{}, {}], [{}, {}]

        def across(h, d):
            up[h][d] = send(h, d, 0, 0, 1)
            down[h][d] = send(h, d, 0, 0, -1)

        def pass_on(h, d):
            up[h][d].wait_recv()
            up2[h][d] = send(h, d, -1, 0, 1, 0)
            down[h][d].wait_recv()
            down2[h][d] = send(h, d, 1, 0, -1, 1)

        for h in range(2):
            along[h][-1] = send(h, 0, 0, 1, 0)
            along[h][1] = send(h, 0, 0, -1, 0)
            across(h, 0)
            along[h][2] = send(h, 0, 0, 2, 0)
        yield
        for d in (-1, 1):
            for h in range(2):
                along[h][d].wait_recv()
                across(h, d)
        for h in range(2):
            pass_on(h, 0)
        for h in range(2):
            along[h][2].wait_recv()
            across(h, 2)
        yield
        for d in (-1, 1, 2):
            for h in range(2):
                pass_on(h, d)
        yield
        for d in (0, -1, 1, 2):
            for h in range(2):
                up2[h][d].wait_recv()
                down2[h][d].wait_recv()

    def scatter_tp(turn, s):
        to_core = remote(part.at[turn, s, 1 - core], from_core.at[turn, s], (g, partner))
        yield
        to_core.wait_recv()
        for k in range(4):
            part[turn, s, core, k] = (
                part[turn, s, core, k].astype(F32) + from_core[turn, s, k].astype(F32)
            ).astype(BF16)
        moves = []
        for i, dx in enumerate((1, -1, 2)):
            chip = lax.rem(x + dx + 4, 4)
            moves.append(
                remote(part.at[turn, s, core, chip], from_x.at[turn, s, i], (g, tp_at(dx)))
            )
        yield
        total = part[turn, s, core, x].astype(F32)
        for i, move in enumerate(moves):
            move.wait_recv()
            total = total + from_x[turn, s, i].astype(F32)
        return total[:, :COLS]

    tables_in.wait()
    block_id = lax.broadcasted_iota(jnp.int32, (1, 384), 1)

    def own_blocks(slot, owners):
        for j in range(BLOCKS):
            owners = jnp.where(block_id == tables[j, slot], slot, owners)
        return owners

    owner_row[...] = lax.fori_loop(0, SLOTS, own_blocks, jnp.zeros((1, 384), jnp.int32), unroll=4)
    owner_in = bring(owner_row, owner)
    for copy in queries_in:
        copy.wait()
    owner_in.wait()

    lane = lax.broadcasted_iota(jnp.int32, (2 * HEADS, 128), 1)

    def one_piece(i, carry):
        piece(i).wait()
        at_ring = lax.rem(i, RING)
        for c in range(PIECE):
            chunk = ring[at_ring, :, c * 128 : c * 128 + 128]
            which = i * PIECE + c
            both = [
                q_ref[owner[0, 2 * which + k]] for k in range(2)
            ]
            both = jnp.dot(
                jnp.concatenate(both, axis=0), chunk, preferred_element_type=F32
            )
            scores[which] = jnp.where(lane < BLOCK, both[: 2 * HEADS], both[2 * HEADS :])
            turned = chunk[:RANK, :].T
            values[2 * which] = turned[:BLOCK]
            values[2 * which + 1] = turned[BLOCK:]

        @pl.when(i + RING < PIECES)
        def _():
            piece(i + RING).start()

        return carry

    lax.fori_loop(0, PIECES, one_piece, 0)
    vup_in = bring(vup_hbm, vup)
    wo = [ring.at[2 + h, pl.ds(0, COLS), pl.ds(0, 1024)] for h in range(2)]
    wo_in = [bring(wo_hbm.at[:, pl.ds(1024 * h, 1024)], wo[h]) for h in range(2)]
    res_in = bring(residual, res)
    wg_in = bring(wg_hbm, wg)
    wu_in = bring(wu_hbm, wu)
    wd = [ring.at[h, pl.ds(0, COLS), pl.ds(0, 1152)] for h in range(2)]
    wd_in = [bring(wd_hbm.at[:, pl.ds(1152 * h, 1152)], wd[h]) for h in range(2)]

    for copy in small:
        copy.wait()
    spread = lax.broadcasted_iota(jnp.int32, (GRPS, GRPS), 1)
    row_of = lax.broadcasted_iota(jnp.int32, (GRPS, GRPS), 0)
    ends = jnp.sum(jnp.where(spread <= row_of, rows_ref[...], 0), axis=1, keepdims=True)
    starts = jnp.sum(jnp.where(spread < row_of, rows_ref[...], 0), axis=1, keepdims=True)
    order = order_ref[...]
    in_group = jnp.logical_and(order >= starts, order < ends)
    group_id = lax.broadcasted_iota(jnp.int32, (GRPS, REQS), 0)
    spot = order - starts
    spot = (spot >> 4) * (GRPS * BATCH) + group_id * BATCH + (spot & 15)
    at = jnp.sum(jnp.where(in_group, spot, 0), axis=0, keepdims=True)
    matches = lax.broadcasted_iota(jnp.int32, (GRPS * SLOTS, REQS), 0) == at
    select[...] = jnp.where(matches, 1.0, 0.0).astype(BF16)
    group_row = lax.broadcasted_iota(jnp.int32, (1, GRPS), 1)
    my_start = jnp.sum(jnp.where(group_row < g, rows_ref[...], 0), axis=1, keepdims=True)
    my_live = jnp.sum(jnp.where(group_row == g, rows_ref[...], 0), axis=1, keepdims=True)
    slot_row = lax.broadcasted_iota(jnp.int32, (SLOTS, REQS), 0)
    named = jnp.logical_and(order - my_start == slot_row, slot_row < my_live)
    slot_len = jnp.sum(jnp.where(named, lengths_ref[...], 0), axis=1, keepdims=True)
    lens[...] = jnp.broadcast_to(slot_len, (SLOTS, 128))
    fresh_all[...] = fresh_ref[...].astype(F32)

    step_of = lax.broadcasted_iota(jnp.int32, (2 * HEADS, 1), 0) // HEADS
    PER = 4

    def some_slots(b, it):
        tiles, picks = [], []
        for k in range(PER):
            slot = b * BATCH + it * PER + k
            q = q_ref[slot].astype(F32)
            length = lens[pl.ds(slot, 1), :]
            mine, rows = [], []
            for j in range(BLOCKS // 2):
                one, two = tables[2 * j, slot], tables[2 * j + 1, slot]
                odd_one, odd_two = lax.rem(one, 2), lax.rem(two, 2)
                two_score = scores[lax.div(two, 2)]
                two_score = jnp.where(
                    lane * 0 + odd_one == odd_two, pltpu.roll(two_score, BLOCK, 1), two_score
                )
                position = lane + BLOCK * odd_one
                position = jnp.where(position < 2 * BLOCK, position, position - 2 * BLOCK)
                tile = jnp.where(position < BLOCK, scores[lax.div(one, 2)], two_score) * score_scale
                mine.append(jnp.where(position + 128 * j < length, tile, -jnp.inf))
                rows.append(values[one + (two - one) * odd_one])
                rows.append(values[two + (one - two) * odd_one])
            new = [fresh_all[n, pl.ds(slot, 1), :] for n in range(2)]
            now = jnp.sum(q * new[0], axis=1, keepdims=True) * score_scale
            later = jnp.sum(q * new[1], axis=1, keepdims=True) * score_scale
            later = jnp.where(step_of == 1, later, -jnp.inf)
            tiles.append((jnp.concatenate(mine, axis=1), now, later, new))
            picks.append(jnp.concatenate(rows, axis=0))
        for k in range(PER):
            tile, now, later, new = tiles[k]
            largest = jnp.maximum(jnp.max(tile, axis=1, keepdims=True), jnp.maximum(now, later))
            expo = jnp.exp(tile - largest)
            now = jnp.exp(now - largest)
            later = jnp.exp(later - largest)
            inverse = 1.0 / (jnp.sum(expo, axis=1, keepdims=True) + now + later)
            mixed = jnp.dot(expo.astype(BF16), picks[k], preferred_element_type=F32)
            mixed = mixed + now * new[0][:, :RANK] + later * new[1][:, :RANK]
            lat[it * PER + k] = mixed * inverse

    def cut_heads(ref, at, half):
        return ref.at[at, :, pl.ds(512 * half, 512)]

    def cut_hidden(ref, at, half):
        return ref.at[at, :, pl.ds(0, 640) if half == 0 else pl.ds(640, 512)]

    part[:, :, :, :, :, 384:] = jnp.zeros(part.shape[:-1] + (128,), BF16)
    first = (pl.ds(0, 1280), pl.ds(0, 1152))
    second = (pl.ds(1280, 1152), pl.ds(1152, 1152))
    rest = pl.ds(0, 1152)
    chunks, weight = (chunks_a, chunks_b), (wg, wu)
    relay, final, line = (relay_a, relay_b), (final_a, final_b), (line_a, line_b)
    final2 = (final2_a, final2_b)

    def along(h, d):
        return (group_at(d, 0) if h == 0 else group_at(0, d), t)

    def across(h, d):
        return along(1 - h, d)

    def product(s, h):
        blocks = []
        for d in range(4):
            for k in range(4):
                b = lax.rem(y + d, 4) * 4 + k if h == 0 else k * 4 + lax.rem(z + d, 4)
                blocks.append(normed[s, b])
        rows = jnp.concatenate(blocks, axis=0)
        if h == 0:
            for d in range(4):
                chunks[h][s, d, :, FFT:] = rows[64 * d : 64 * d + 64, 384:]
        rows = rows[:, :COLS]
        for n in range(3):
            at = slice(768 * n, 768 * n + 768)
            value = jnp.dot(rows, weight[h][:, at], preferred_element_type=F32).astype(BF16)
            for d in range(4):
                chunks[h][s, d, :, at] = value[64 * d : 64 * d + 64]

    def add(ref, s, index, columns, other):
        ref[s, index, :, columns] = (
            ref[s, index, :, columns].astype(F32) + other[...].astype(F32)
        ).astype(BF16)

    def after_heads(s):
        if s == 0:
            for copy in wo_in:
                copy.wait()
        rows = []
        for b in range(BATCHES):
            both = [gathered[h, s, b].reshape(GRPS * BATCH, 1024) for h in range(2)]
            value = lax.dot_general(both[0], wo[0][...], NT, preferred_element_type=F32)
            value = value + lax.dot_general(both[1], wo[1][...], NT, preferred_element_type=F32)
            rows.append(value.astype(BF16))
        value = jnp.concatenate(rows, axis=0)
        placed = lax.dot_general(select[...], value, TN, preferred_element_type=F32).astype(BF16)
        for k in range(8):
            part[0, s, k % 2, k // 2, :, :COLS] = placed[32 * k : 32 * k + 32]
        attention = yield from scatter_tp(0, s)

        if s == 0:
            res_in.wait()
        mine = lax.broadcasted_iota(jnp.int32, (32, REQS), 1) == (
            lax.broadcasted_iota(jnp.int32, (32, REQS), 0) + t * 32
        )
        mine = jnp.where(mine, 1.0, 0.0).astype(BF16)
        here = lax.dot_general(mine, res[s], NT, preferred_element_type=F32) + attention
        stream[s] = here
        squares = jnp.sum(here * here, axis=1, keepdims=True)
        high = squares.astype(BF16)
        low = (squares - high.astype(F32)).astype(BF16)
        extra_lane = lax.broadcasted_iota(jnp.int32, (32, WIDE - COLS), 1)
        extra = jnp.where(
            extra_lane == 0, high, jnp.where(extra_lane == 1, low, jnp.zeros_like(high))
        )
        scaled = (here * gain_ref[...].reshape(1, COLS).astype(F32)).astype(BF16)
        scaled = jnp.concatenate([scaled, extra], axis=1)
        normed[s, 2 * t] = scaled[:16]
        normed[s, 2 * t + 1] = scaled[16:]

        def pair(index):
            return normed.at[s, pl.ds(2 * index, 2)]

        moves = [remote(pair(t), pair(t), (g, tp_at(dx))) for dx in (1, -1, 2)]
        moves.append(remote(pair(t), pair(t), (g, partner)))
        yield
        shares = []
        for move, dx in zip(moves[:3], (-1, 1, 2)):
            move.wait_recv()
            shares.append(remote(pair(tp_at(dx)), pair(tp_at(dx)), (g, partner)))
        yield
        for move in moves[3:] + shares:
            move.wait_recv()
        if s == 0:
            wg_in.wait()
            wu_in.wait()

        relays, finals, finals2 = [None, None], [[], []], [[], []]
        for h in range(2):
            product(s, h)
            relays[h] = (
                remote(
                    chunks[h].at[s, 2, :, first[h]], relay[h].at[s, 0, :, first[h]], along(h, 1)
                ),
                remote(chunks[h].at[s, 2, :, second[h]], relay[h].at[s, 1, :, rest], along(h, -1)),
            )
            finals[h].append(
                remote(
                    chunks[h].at[s, 1, :, second[h]], final[h].at[s, 0, :, second[h]], along(h, 1)
                )
            )
            finals[h].append(
                remote(
                    chunks[h].at[s, 3, :, first[h]], final[h].at[s, 1, :, first[h]], along(h, -1)
                )
            )
        yield
        for h in range(2):
            relays[h][0].wait_recv()
            add(chunks[h], s, 1, first[h], relay[h].at[s, 0, :, first[h]])
            finals[h].append(
                remote(
                    chunks[h].at[s, 1, :, first[h]], final[h].at[s, 0, :, first[h]], along(h, 1)
                )
            )
            relays[h][1].wait_recv()
            add(chunks[h], s, 3, second[h], relay[h].at[s, 1, :, rest])
            finals[h].append(
                remote(
                    chunks[h].at[s, 3, :, second[h]], final[h].at[s, 1, :, second[h]], along(h, -1)
                )
            )
        yield
        for h in range(2):
            for copy in finals[h]:
                copy.wait_recv()
            for k in range(4):
                at = pl.ds(16 * k, 16)
                line[h][s, k] = (
                    chunks[h][s, 0, at, :].astype(F32)
                    + final[h][s, 0, at, :].astype(F32)
                    + final[h][s, 1, at, :].astype(F32)
                ).astype(BF16)
            place = z if h == 0 else y
            for i, d in enumerate((1, -1, 2)):
                block = line[h].at[s, lax.rem(place + d + 4, 4)]
                finals2[h].append(remote(block, final2[h].at[s, i], across(h, d)))
        yield
        totals = []
        for h in range(2):
            for copy in finals2[h]:
                copy.wait_recv()
            place = z if h == 0 else y
            totals.append(
                line[h][s, place].astype(F32)
                + final2[h][s, 0].astype(F32)
                + final2[h][s, 1].astype(F32)
                + final2[h][s, 2].astype(F32)
            )
        mean = (totals[0][:, FFT + 64 : FFT + 65] + totals[0][:, FFT + 65 : FFT + 66]) / D
        inverse_rms = lax.rsqrt(mean + 1e-06)
        gate = totals[0][:, :FFT] * inverse_rms
        up = totals[1] * inverse_rms
        hidden = (gate / (1.0 + jnp.exp(-gate)) * up).astype(BF16)
        for h in range(2):
            hiddens[h, s, g] = hidden[:, 1152 * h : 1152 * h + 1152]
        yield from all_gather([hiddens.at[h, s] for h in range(2)], cut_hidden)

        if s == 0:
            for copy in wd_in:
                copy.wait()
        both = [hiddens[h, s].reshape(REQS, 1152) for h in range(2)]
        value = lax.dot_general(both[0], wd[0][...], NT, preferred_element_type=F32)
        value = value + lax.dot_general(both[1], wd[1][...], NT, preferred_element_type=F32)
        value = value.astype(BF16)
        for k in range(8):
            part[1, s, k % 2, k // 2, :, :COLS] = value[32 * k : 32 * k + 32]
        reduced = yield from scatter_tp(1, s)
        out_ref[s] = (stream[s] + reduced).astype(BF16)

    def slots(b, low, high):
        def one_step(it, carry):
            some_slots(b, it)
            return carry

        lax.fori_loop(low, high, one_step, 0)

    def raise_values(b):
        for h in range(HEADS):
            both = jnp.concatenate([lat[:, h, :], lat[:, HEADS + h, :]], axis=0).astype(BF16)
            value = jnp.dot(both, vup[h], preferred_element_type=F32).astype(BF16)
            for s in range(2):
                gathered[h // 8, s, b, g, :, (h % 8) * VH : (h % 8 + 1) * VH] = value[
                    BATCH * s : BATCH * s + BATCH
                ]

    heads = [
        [all_gather([gathered.at[h, s, b] for h in range(2)], cut_heads) for b in range(2)]
        for s in range(2)
    ]
    late = [after_heads(s) for s in range(2)]

    def go(*turns):
        for one in turns:
            next(one, None)

    slots(0, 0, 4)
    vup_in.wait()
    raise_values(0)
    pl.semaphore_wait(barrier, len(greet))
    go(heads[0][0])
    slots(1, 0, 1)
    go(heads[1][0])
    slots(1, 1, 2)
    go(heads[0][0])
    slots(1, 2, 3)
    go(heads[1][0])
    slots(1, 3, 4)
    raise_values(1)
    go(heads[0][1], heads[0][0], heads[0][1], heads[1][1], heads[0][0])
    go(heads[0][1], heads[1][0], heads[0][1])
    go(late[0], heads[1][1], heads[1][0])
    go(late[0], heads[1][1])
    go(late[0], heads[1][1])
    go(late[0], late[0])
    go(late[1], late[0], late[1], late[1], late[1], late[1])
    for _ in range(7):
        go(late[0], late[1])
    go(late[1])
    for copy in used:
        copy.wait_send()


def layer(
    queries,
    new_latent,
    latent_cache,
    tables,
    context_len,
    group_rows,
    request_order,
    residual,
    value_up,
    out_proj,
    norm_gain,
    gate_proj,
    up_proj,
    down_proj,
):
    hbm = pl.BlockSpec(memory_space=pl.ANY)
    copies = 4 * 38 + 2 * 38 + 4 * 4 + 2 * 7 + 2 * 18
    return pl.pallas_call(
        layer_kernel,
        out_shape=jax.ShapeDtypeStruct((2, 32, COLS), BF16),
        in_specs=[hbm] * 14,
        out_specs=pl.BlockSpec(memory_space=pltpu.VMEM),
        scratch_shapes=[
            pltpu.VMEM((SLOTS, 2 * HEADS, KDIM), BF16),
            pltpu.VMEM((2, SLOTS, KDIM), BF16),
            pltpu.VMEM((2, SLOTS, KDIM), F32),
            pltpu.SMEM((BLOCKS, SLOTS), jnp.int32),
            pltpu.VMEM((1, REQS), jnp.int32),
            pltpu.VMEM((1, GRPS), jnp.int32),
            pltpu.VMEM((1, REQS), jnp.int32),
            pltpu.VMEM((COLS,), BF16),
            pltpu.VMEM((HEADS, RANK, VH), BF16),
            pltpu.VMEM((RING, KDIM, PIECE * 128), BF16),
            pltpu.VMEM((POOL, BLOCK, RANK), BF16),
            pltpu.VMEM((POOL // 2, 2 * HEADS, 128), F32),
            pltpu.VMEM((BATCH, 2 * HEADS, RANK), F32),
            pltpu.VMEM((SLOTS, 128), jnp.int32),
            pltpu.VMEM((1, 384), jnp.int32),
            pltpu.SMEM((1, 384), jnp.int32),
            pltpu.SemaphoreType.DMA((RING,)),
            pltpu.VMEM((COLS, FFT), BF16),
            pltpu.VMEM((COLS, FFT), BF16),
            pltpu.VMEM((2, COLS, REQS), BF16),
            pltpu.VMEM((2, 2, BATCHES, GRPS, BATCH, 1024), BF16),
            pltpu.VMEM((2, 2, GRPS, 16, 1152), BF16),
            pltpu.VMEM((GRPS * SLOTS, REQS), BF16),
            pltpu.VMEM((2, 32, COLS), F32),
            pltpu.VMEM((2, 2, 2, 4, 32, WIDE), BF16),
            pltpu.VMEM((2, 2, 4, 32, WIDE), BF16),
            pltpu.VMEM((2, 2, 3, 32, WIDE), BF16),
            pltpu.VMEM((2, 16, 16, WIDE), BF16),
            pltpu.VMEM((2, 4, 64, FFT + TAIL), BF16),
            pltpu.VMEM((2, 4, 64, FFT), BF16),
            pltpu.VMEM((2, 2, 64, 1280), BF16),
            pltpu.VMEM((2, 2, 64, 1152), BF16),
            pltpu.VMEM((2, 2, 64, FFT + TAIL), BF16),
            pltpu.VMEM((2, 2, 64, FFT), BF16),
            pltpu.VMEM((2, 4, 16, FFT + TAIL), BF16),
            pltpu.VMEM((2, 4, 16, FFT), BF16),
            pltpu.VMEM((2, 3, 16, FFT + TAIL), BF16),
            pltpu.VMEM((2, 3, 16, FFT), BF16),
            pltpu.SemaphoreType.DMA((17,)),
            pltpu.SemaphoreType.DMA((copies,)),
            pltpu.SemaphoreType.DMA((copies,)),
        ],
        compiler_params=pltpu.CompilerParams(
            collective_id=0, has_side_effects=True, vmem_limit_bytes=63 << 20
        ),
    )(
        queries,
        new_latent,
        latent_cache.T,
        tables.T,
        context_len.reshape(1, REQS),
        group_rows.reshape(1, GRPS),
        request_order.reshape(1, REQS),
        jnp.swapaxes(residual, 1, 2),
        norm_gain,
        value_up,
        out_proj.T,
        gate_proj,
        up_proj,
        down_proj.T,
    )


def solution(mesh):
    placed = (
        P(None, "grp", "tp", None),
        P(None, "grp", None),
        P("grp", None),
        P("grp", None),
        P(),
        P(),
        P(),
        P(None, None, "grp"),
        P("tp", None, None),
        P("tp", "grp"),
        P("grp"),
        P("grp", "tp"),
        P("grp", "tp"),
        P("tp", "grp"),
    )
    return jax.shard_map(
        layer, mesh=mesh, in_specs=placed, out_specs=P(None, "tp", "grp"), check_vma=False
    )
```

```python
import jax
import jax.numpy as jnp
from jax import lax
from jax.experimental import pallas as pl
from jax.experimental.pallas import tpu as pltpu
from jax.sharding import PartitionSpec as P

D = 7168
SLOTS = 32
BLOCKS = 10
BLOCK = 64
HEADS = 16
KDIM = 576
RANK = 512
VH = 128
GRPS = 16
REQS = 256
POOL = 320
BATCH = 16
BATCHES = SLOTS // BATCH
PIECE = 10
PIECES = POOL // 2 // PIECE
RING = 4

score_scale = 192.0 ** (-0.5)
NT = (((1,), (1,)), ((), ()))
TN = (((0,), (0,)), ((), ()))

MESH = pl.DeviceIdType.MESH
WIDE = 512
COLS = 448
FFT = 2304
TAIL = 128
BF16 = jnp.bfloat16
F32 = jnp.float32


def layer_kernel(
    queries,
    fresh_hbm,
    cache,
    tables_hbm,
    lengths_hbm,
    rows_hbm,
    order_hbm,
    residual,
    gain_hbm,
    vup_hbm,
    wo_hbm,
    wg_hbm,
    wu_hbm,
    wd_hbm,
    out_ref,
    q_ref,
    fresh_ref,
    fresh_all,
    tables,
    lengths_ref,
    rows_ref,
    order_ref,
    gain_ref,
    vup,
    ring,
    values,
    scores,
    lat,
    lens,
    owner_row,
    owner,
    ring_sems,
    wg,
    wu,
    res,
    gathered,
    hiddens,
    select,
    stream,
    part,
    from_core,
    from_x,
    normed,
    chunks_a,
    chunks_b,
    relay_a,
    relay_b,
    final_a,
    final_b,
    line_a,
    line_b,
    final2_a,
    final2_b,
    local_sems,
    send_sems,
    recv_sems,
):
    g, t = lax.axis_index("grp"), lax.axis_index("tp")
    y, z = g // 4, lax.rem(g, 4)
    x, core = t // 2, lax.rem(t, 2)

    def group_at(dy, dz):
        return lax.rem(y + dy + 4, 4) * 4 + lax.rem(z + dz + 4, 4)

    def tp_at(dx):
        return lax.rem(x + dx + 4, 4) * 2 + core

    partner = x * 2 + 1 - core
    used = []

    def remote(src, dst, device):
        i = len(used)
        copy = pltpu.make_async_remote_copy(
            src_ref=src,
            dst_ref=dst,
            send_sem=send_sems.at[i],
            recv_sem=recv_sems.at[i],
            device_id=device,
            device_id_type=MESH,
        )
        copy.start()
        used.append(copy)
        return copy

    local = []

    def bring(src, dst):
        copy = pltpu.make_async_copy(src, dst, local_sems.at[len(local)])
        copy.start()
        local.append(copy)
        return copy

    def piece(i):
        at = pl.ds(pl.multiple_of(i * PIECE * 128, PIECE * 128), PIECE * 128)
        at_ring = lax.rem(i, RING)
        return pltpu.make_async_copy(cache.at[:, at], ring.at[at_ring], ring_sems.at[at_ring])

    tables_in = bring(tables_hbm, tables)
    queries_in = [
        bring(queries.at[0], q_ref.at[:, pl.ds(0, HEADS)]),
        bring(queries.at[1], q_ref.at[:, pl.ds(HEADS, HEADS)]),
    ]
    for i in range(RING):
        piece(i).start()
    small = [
        bring(fresh_hbm, fresh_ref),
        bring(lengths_hbm, lengths_ref),
        bring(rows_hbm, rows_ref),
        bring(order_hbm, order_ref),
        bring(gain_hbm, gain_ref),
    ]

    barrier = pltpu.get_barrier_semaphore()
    greet = [(group_at(dy, dz), t) for dy, dz in ((1, 0), (-1, 0), (2, 0), (0, 1), (0, -1), (0, 2))]
    greet += [(g, tp_at(1)), (g, tp_at(-1)), (g, tp_at(2)), (g, partner)]
    for device in greet:
        pl.semaphore_signal(barrier, inc=1, device_id=device, device_id_type=MESH)

    def all_gather(bufs, cut):
        def slot(h, da, db):
            return group_at(da, db) if h == 0 else group_at(db, da)

        def send(h, da, db, to_a, to_b, half=None):
            at = slot(h, da, db)
            ref = bufs[h].at[at] if half is None else cut(bufs[h], at, half)
            return remote(ref, ref, (slot(h, to_a, to_b), t))

        along = [{}, {}]
        up, down, up2, down2 = [{}, {}], [{}, {}], [{}, {}], [{}, {}]

        def across(h, d):
            up[h][d] = send(h, d, 0, 0, 1)
            down[h][d] = send(h, d, 0, 0, -1)

        def pass_on(h, d):
            up[h][d].wait_recv()
            up2[h][d] = send(h, d, -1, 0, 1, 0)
            down[h][d].wait_recv()
            down2[h][d] = send(h, d, 1, 0, -1, 1)

        for h in range(2):
            along[h][-1] = send(h, 0, 0, 1, 0)
            along[h][1] = send(h, 0, 0, -1, 0)
            across(h, 0)
            along[h][2] = send(h, 0, 0, 2, 0)
        yield
        for d in (-1, 1):
            for h in range(2):
                along[h][d].wait_recv()
                across(h, d)
        for h in range(2):
            pass_on(h, 0)
        for h in range(2):
            along[h][2].wait_recv()
            across(h, 2)
        yield
        for d in (-1, 1, 2):
            for h in range(2):
                pass_on(h, d)
        yield
        for d in (0, -1, 1, 2):
            for h in range(2):
                up2[h][d].wait_recv()
                down2[h][d].wait_recv()

    def scatter_tp(turn, s):
        to_core = remote(part.at[turn, s, 1 - core], from_core.at[turn, s], (g, partner))
        yield
        to_core.wait_recv()
        for k in range(4):
            part[turn, s, core, k] = (
                part[turn, s, core, k].astype(F32) + from_core[turn, s, k].astype(F32)
            ).astype(BF16)
        moves = []
        for i, dx in enumerate((1, -1, 2)):
            chip = lax.rem(x + dx + 4, 4)
            moves.append(
                remote(part.at[turn, s, core, chip], from_x.at[turn, s, i], (g, tp_at(dx)))
            )
        yield
        total = part[turn, s, core, x].astype(F32)
        for i, move in enumerate(moves):
            move.wait_recv()
            total = total + from_x[turn, s, i].astype(F32)
        return total[:, :COLS]

    tables_in.wait()
    block_id = lax.broadcasted_iota(jnp.int32, (1, 384), 1)

    def own_blocks(slot, owners):
        for j in range(BLOCKS):
            owners = jnp.where(block_id == tables[j, slot], slot, owners)
        return owners

    owner_row[...] = lax.fori_loop(0, SLOTS, own_blocks, jnp.zeros((1, 384), jnp.int32), unroll=4)
    owner_in = bring(owner_row, owner)
    for copy in queries_in:
        copy.wait()
    owner_in.wait()

    lane = lax.broadcasted_iota(jnp.int32, (2 * HEADS, 128), 1)

    def one_piece(i, carry):
        piece(i).wait()
        at_ring = lax.rem(i, RING)
        for c in range(PIECE):
            chunk = ring[at_ring, :, c * 128 : c * 128 + 128]
            which = i * PIECE + c
            both = [
                q_ref[owner[0, 2 * which + k]] for k in range(2)
            ]
            both = jnp.dot(
                jnp.concatenate(both, axis=0), chunk, preferred_element_type=F32
            )
            scores[which] = jnp.where(lane < BLOCK, both[: 2 * HEADS], both[2 * HEADS :])
            turned = chunk[:RANK, :].T
            values[2 * which] = turned[:BLOCK]
            values[2 * which + 1] = turned[BLOCK:]

        @pl.when(i + RING < PIECES)
        def _():
            piece(i + RING).start()

        return carry

    lax.fori_loop(0, PIECES, one_piece, 0)
    vup_in = bring(vup_hbm, vup)
    wo = [ring.at[2 + h, pl.ds(0, COLS), pl.ds(0, 1024)] for h in range(2)]
    wo_in = [bring(wo_hbm.at[:, pl.ds(1024 * h, 1024)], wo[h]) for h in range(2)]
    res_in = bring(residual, res)
    wg_in = bring(wg_hbm, wg)
    wu_in = bring(wu_hbm, wu)
    wd = [ring.at[h, pl.ds(0, COLS), pl.ds(0, 1152)] for h in range(2)]
    wd_in = [bring(wd_hbm.at[:, pl.ds(1152 * h, 1152)], wd[h]) for h in range(2)]

    for copy in small:
        copy.wait()
    order = order_ref[...]
    group_row = lax.broadcasted_iota(jnp.int32, (1, GRPS), 1)
    my_start = jnp.sum(jnp.where(group_row < g, rows_ref[...], 0), axis=1, keepdims=True)
    my_live = jnp.sum(jnp.where(group_row == g, rows_ref[...], 0), axis=1, keepdims=True)
    slot_row = lax.broadcasted_iota(jnp.int32, (SLOTS, REQS), 0)
    named = jnp.logical_and(order - my_start == slot_row, slot_row < my_live)
    slot_len = jnp.sum(jnp.where(named, lengths_ref[...], 0), axis=1, keepdims=True)
    lens[...] = jnp.broadcast_to(slot_len, (SLOTS, 128))
    fresh_all[...] = fresh_ref[...].astype(F32)

    step_of = lax.broadcasted_iota(jnp.int32, (2 * HEADS, 1), 0) // HEADS
    PER = 4

    def some_slots(b, it):
        tiles, picks = [], []
        for k in range(PER):
            slot = b * BATCH + it * PER + k
            q = q_ref[slot].astype(F32)
            length = lens[pl.ds(slot, 1), :]
            mine, rows = [], []
            for j in range(BLOCKS // 2):
                one, two = tables[2 * j, slot], tables[2 * j + 1, slot]
                odd_one, odd_two = lax.rem(one, 2), lax.rem(two, 2)
                two_score = scores[lax.div(two, 2)]
                two_score = jnp.where(
                    lane * 0 + odd_one == odd_two, pltpu.roll(two_score, BLOCK, 1), two_score
                )
                position = lane + BLOCK * odd_one
                position = jnp.where(position < 2 * BLOCK, position, position - 2 * BLOCK)
                tile = jnp.where(position < BLOCK, scores[lax.div(one, 2)], two_score) * score_scale
                mine.append(jnp.where(position + 128 * j < length, tile, -jnp.inf))
                rows.append(values[one + (two - one) * odd_one])
                rows.append(values[two + (one - two) * odd_one])
            new = [fresh_all[n, pl.ds(slot, 1), :] for n in range(2)]
            now = jnp.sum(q * new[0], axis=1, keepdims=True) * score_scale
            later = jnp.sum(q * new[1], axis=1, keepdims=True) * score_scale
            later = jnp.where(step_of == 1, later, -jnp.inf)
            tiles.append((jnp.concatenate(mine, axis=1), now, later, new))
            picks.append(jnp.concatenate(rows, axis=0))
        for k in range(PER):
            tile, now, later, new = tiles[k]
            largest = jnp.maximum(jnp.max(tile, axis=1, keepdims=True), jnp.maximum(now, later))
            expo = jnp.exp(tile - largest)
            now = jnp.exp(now - largest)
            later = jnp.exp(later - largest)
            inverse = 1.0 / (jnp.sum(expo, axis=1, keepdims=True) + now + later)
            mixed = jnp.dot(expo.astype(BF16), picks[k], preferred_element_type=F32)
            mixed = mixed + now * new[0][:, :RANK] + later * new[1][:, :RANK]
            lat[it * PER + k] = mixed * inverse

    def cut_heads(ref, at, half):
        return ref.at[at, :, pl.ds(512 * half, 512)]

    def cut_hidden(ref, at, half):
        return ref.at[at, :, pl.ds(0, 640) if half == 0 else pl.ds(640, 512)]

    part[:, :, :, :, :, 384:] = jnp.zeros(part.shape[:-1] + (128,), BF16)
    first = (pl.ds(0, 1280), pl.ds(0, 1152))
    second = (pl.ds(1280, 1152), pl.ds(1152, 1152))
    rest = pl.ds(0, 1152)
    chunks, weight = (chunks_a, chunks_b), (wg, wu)
    relay, final, line = (relay_a, relay_b), (final_a, final_b), (line_a, line_b)
    final2 = (final2_a, final2_b)

    def along(h, d):
        return (group_at(d, 0) if h == 0 else group_at(0, d), t)

    def across(h, d):
        return along(1 - h, d)

    def product(s, h):
        blocks = []
        for d in range(4):
            for k in range(4):
                b = lax.rem(y + d, 4) * 4 + k if h == 0 else k * 4 + lax.rem(z + d, 4)
                blocks.append(normed[s, b])
        rows = jnp.concatenate(blocks, axis=0)
        if h == 0:
            for d in range(4):
                chunks[h][s, d, :, FFT:] = rows[64 * d : 64 * d + 64, 384:]
        rows = rows[:, :COLS]
        for n in range(3):
            at = slice(768 * n, 768 * n + 768)
            value = jnp.dot(rows, weight[h][:, at], preferred_element_type=F32).astype(BF16)
            for d in range(4):
                chunks[h][s, d, :, at] = value[64 * d : 64 * d + 64]

    def add(ref, s, index, columns, other):
        ref[s, index, :, columns] = (
            ref[s, index, :, columns].astype(F32) + other[...].astype(F32)
        ).astype(BF16)

    def after_heads(s):
        if s == 0:
            for copy in wo_in:
                copy.wait()
        rows = []
        for b in range(BATCHES):
            both = [gathered[h, s, b].reshape(GRPS * BATCH, 1024) for h in range(2)]
            value = lax.dot_general(both[0], wo[0][...], NT, preferred_element_type=F32)
            value = value + lax.dot_general(both[1], wo[1][...], NT, preferred_element_type=F32)
            rows.append(value.astype(BF16))
        value = jnp.concatenate(rows, axis=0)
        placed = lax.dot_general(select[...], value, TN, preferred_element_type=F32).astype(BF16)
        for k in range(8):
            part[0, s, k % 2, k // 2, :, :COLS] = placed[32 * k : 32 * k + 32]
        attention = yield from scatter_tp(0, s)

        if s == 0:
            res_in.wait()
        mine = lax.broadcasted_iota(jnp.int32, (32, REQS), 1) == (
            lax.broadcasted_iota(jnp.int32, (32, REQS), 0) + t * 32
        )
        mine = jnp.where(mine, 1.0, 0.0).astype(BF16)
        here = lax.dot_general(mine, res[s], NT, preferred_element_type=F32) + attention
        stream[s] = here
        squares = jnp.sum(here * here, axis=1, keepdims=True)
        high = squares.astype(BF16)
        low = (squares - high.astype(F32)).astype(BF16)
        extra_lane = lax.broadcasted_iota(jnp.int32, (32, WIDE - COLS), 1)
        extra = jnp.where(
            extra_lane == 0, high, jnp.where(extra_lane == 1, low, jnp.zeros_like(high))
        )
        scaled = (here * gain_ref[...].reshape(1, COLS).astype(F32)).astype(BF16)
        scaled = jnp.concatenate([scaled, extra], axis=1)
        normed[s, 2 * t] = scaled[:16]
        normed[s, 2 * t + 1] = scaled[16:]

        def pair(index):
            return normed.at[s, pl.ds(2 * index, 2)]

        moves = [remote(pair(t), pair(t), (g, tp_at(dx))) for dx in (1, -1, 2)]
        moves.append(remote(pair(t), pair(t), (g, partner)))
        yield
        shares = []
        for move, dx in zip(moves[:3], (-1, 1, 2)):
            move.wait_recv()
            shares.append(remote(pair(tp_at(dx)), pair(tp_at(dx)), (g, partner)))
        yield
        for move in moves[3:] + shares:
            move.wait_recv()
        if s == 0:
            wg_in.wait()
            wu_in.wait()

        relays, finals, finals2 = [None, None], [[], []], [[], []]
        for h in range(2):
            product(s, h)
            relays[h] = (
                remote(
                    chunks[h].at[s, 2, :, first[h]], relay[h].at[s, 0, :, first[h]], along(h, 1)
                ),
                remote(chunks[h].at[s, 2, :, second[h]], relay[h].at[s, 1, :, rest], along(h, -1)),
            )
            finals[h].append(
                remote(
                    chunks[h].at[s, 1, :, second[h]], final[h].at[s, 0, :, second[h]], along(h, 1)
                )
            )
            finals[h].append(
                remote(
                    chunks[h].at[s, 3, :, first[h]], final[h].at[s, 1, :, first[h]], along(h, -1)
                )
            )
        yield
        for h in range(2):
            relays[h][0].wait_recv()
            add(chunks[h], s, 1, first[h], relay[h].at[s, 0, :, first[h]])
            finals[h].append(
                remote(
                    chunks[h].at[s, 1, :, first[h]], final[h].at[s, 0, :, first[h]], along(h, 1)
                )
            )
            relays[h][1].wait_recv()
            add(chunks[h], s, 3, second[h], relay[h].at[s, 1, :, rest])
            finals[h].append(
                remote(
                    chunks[h].at[s, 3, :, second[h]], final[h].at[s, 1, :, second[h]], along(h, -1)
                )
            )
        yield
        for h in range(2):
            for copy in finals[h]:
                copy.wait_recv()
            for k in range(4):
                at = pl.ds(16 * k, 16)
                line[h][s, k] = (
                    chunks[h][s, 0, at, :].astype(F32)
                    + final[h][s, 0, at, :].astype(F32)
                    + final[h][s, 1, at, :].astype(F32)
                ).astype(BF16)
            place = z if h == 0 else y
            for i, d in enumerate((1, -1, 2)):
                block = line[h].at[s, lax.rem(place + d + 4, 4)]
                finals2[h].append(remote(block, final2[h].at[s, i], across(h, d)))
        yield
        totals = []
        for h in range(2):
            for copy in finals2[h]:
                copy.wait_recv()
            place = z if h == 0 else y
            totals.append(
                line[h][s, place].astype(F32)
                + final2[h][s, 0].astype(F32)
                + final2[h][s, 1].astype(F32)
                + final2[h][s, 2].astype(F32)
            )
        mean = (totals[0][:, FFT + 64 : FFT + 65] + totals[0][:, FFT + 65 : FFT + 66]) / D
        inverse_rms = lax.rsqrt(mean + 1e-06)
        gate = totals[0][:, :FFT] * inverse_rms
        up = totals[1] * inverse_rms
        hidden = (gate / (1.0 + jnp.exp(-gate)) * up).astype(BF16)
        for h in range(2):
            hiddens[h, s, g] = hidden[:, 1152 * h : 1152 * h + 1152]
        yield from all_gather([hiddens.at[h, s] for h in range(2)], cut_hidden)

        if s == 0:
            for copy in wd_in:
                copy.wait()
        both = [hiddens[h, s].reshape(REQS, 1152) for h in range(2)]
        value = lax.dot_general(both[0], wd[0][...], NT, preferred_element_type=F32)
        value = value + lax.dot_general(both[1], wd[1][...], NT, preferred_element_type=F32)
        value = value.astype(BF16)
        for k in range(8):
            part[1, s, k % 2, k // 2, :, :COLS] = value[32 * k : 32 * k + 32]
        reduced = yield from scatter_tp(1, s)
        out_ref[s] = (stream[s] + reduced).astype(BF16)

    def slots(b, low, high):
        def one_step(it, carry):
            some_slots(b, it)
            return carry

        lax.fori_loop(low, high, one_step, 0)

    def raise_values(b):
        for h in range(HEADS):
            both = jnp.concatenate([lat[:, h, :], lat[:, HEADS + h, :]], axis=0).astype(BF16)
            value = jnp.dot(both, vup[h], preferred_element_type=F32).astype(BF16)
            for s in range(2):
                gathered[h // 8, s, b, g, :, (h % 8) * VH : (h % 8 + 1) * VH] = value[
                    BATCH * s : BATCH * s + BATCH
                ]

    heads = [
        [all_gather([gathered.at[h, s, b] for h in range(2)], cut_heads) for b in range(2)]
        for s in range(2)
    ]
    late = [after_heads(s) for s in range(2)]

    def go(*turns):
        for one in turns:
            next(one, None)

    slots(0, 0, 4)
    vup_in.wait()
    raise_values(0)
    pl.semaphore_wait(barrier, len(greet))
    go(heads[0][0])
    slots(1, 0, 1)
    go(heads[1][0])
    slots(1, 1, 2)
    go(heads[0][0])
    slots(1, 2, 3)
    go(heads[1][0])
    slots(1, 3, 4)
    raise_values(1)
    go(heads[0][1], heads[0][0], heads[0][1], heads[1][1], heads[0][0])
    spread = lax.broadcasted_iota(jnp.int32, (GRPS, GRPS), 1)
    row_of = lax.broadcasted_iota(jnp.int32, (GRPS, GRPS), 0)
    ends = jnp.sum(jnp.where(spread <= row_of, rows_ref[...], 0), axis=1, keepdims=True)
    starts = jnp.sum(jnp.where(spread < row_of, rows_ref[...], 0), axis=1, keepdims=True)
    in_group = jnp.logical_and(order >= starts, order < ends)
    group_id = lax.broadcasted_iota(jnp.int32, (GRPS, REQS), 0)
    spot = order - starts
    spot = (spot >> 4) * (GRPS * BATCH) + group_id * BATCH + (spot & 15)
    at = jnp.sum(jnp.where(in_group, spot, 0), axis=0, keepdims=True)
    matches = lax.broadcasted_iota(jnp.int32, (GRPS * SLOTS, REQS), 0) == at
    select[...] = jnp.where(matches, 1.0, 0.0).astype(BF16)
    go(heads[0][1], heads[1][0], heads[0][1])
    go(late[0], heads[1][1], heads[1][0])
    go(late[0], heads[1][1])
    go(late[0], heads[1][1])
    go(late[0], late[0])
    go(late[1], late[0], late[1], late[1], late[1], late[1])
    for _ in range(7):
        go(late[0], late[1])
    go(late[1])
    for copy in used:
        copy.wait_send()


def layer(
    queries,
    new_latent,
    latent_cache,
    tables,
    context_len,
    group_rows,
    request_order,
    residual,
    value_up,
    out_proj,
    norm_gain,
    gate_proj,
    up_proj,
    down_proj,
):
    hbm = pl.BlockSpec(memory_space=pl.ANY)
    copies = 4 * 38 + 2 * 38 + 4 * 4 + 2 * 7 + 2 * 18
    return pl.pallas_call(
        layer_kernel,
        out_shape=jax.ShapeDtypeStruct((2, 32, COLS), BF16),
        in_specs=[hbm] * 14,
        out_specs=pl.BlockSpec(memory_space=pltpu.VMEM),
        scratch_shapes=[
            pltpu.VMEM((SLOTS, 2 * HEADS, KDIM), BF16),
            pltpu.VMEM((2, SLOTS, KDIM), BF16),
            pltpu.VMEM((2, SLOTS, KDIM), F32),
            pltpu.SMEM((BLOCKS, SLOTS), jnp.int32),
            pltpu.VMEM((1, REQS), jnp.int32),
            pltpu.VMEM((1, GRPS), jnp.int32),
            pltpu.VMEM((1, REQS), jnp.int32),
            pltpu.VMEM((COLS,), BF16),
            pltpu.VMEM((HEADS, RANK, VH), BF16),
            pltpu.VMEM((RING, KDIM, PIECE * 128), BF16),
            pltpu.VMEM((POOL, BLOCK, RANK), BF16),
            pltpu.VMEM((POOL // 2, 2 * HEADS, 128), F32),
            pltpu.VMEM((BATCH, 2 * HEADS, RANK), F32),
            pltpu.VMEM((SLOTS, 128), jnp.int32),
            pltpu.VMEM((1, 384), jnp.int32),
            pltpu.SMEM((1, 384), jnp.int32),
            pltpu.SemaphoreType.DMA((RING,)),
            pltpu.VMEM((COLS, FFT), BF16),
            pltpu.VMEM((COLS, FFT), BF16),
            pltpu.VMEM((2, COLS, REQS), BF16),
            pltpu.VMEM((2, 2, BATCHES, GRPS, BATCH, 1024), BF16),
            pltpu.VMEM((2, 2, GRPS, 16, 1152), BF16),
            pltpu.VMEM((GRPS * SLOTS, REQS), BF16),
            pltpu.VMEM((2, 32, COLS), F32),
            pltpu.VMEM((2, 2, 2, 4, 32, WIDE), BF16),
            pltpu.VMEM((2, 2, 4, 32, WIDE), BF16),
            pltpu.VMEM((2, 2, 3, 32, WIDE), BF16),
            pltpu.VMEM((2, 16, 16, WIDE), BF16),
            pltpu.VMEM((2, 4, 64, FFT + TAIL), BF16),
            pltpu.VMEM((2, 4, 64, FFT), BF16),
            pltpu.VMEM((2, 2, 64, 1280), BF16),
            pltpu.VMEM((2, 2, 64, 1152), BF16),
            pltpu.VMEM((2, 2, 64, FFT + TAIL), BF16),
            pltpu.VMEM((2, 2, 64, FFT), BF16),
            pltpu.VMEM((2, 4, 16, FFT + TAIL), BF16),
            pltpu.VMEM((2, 4, 16, FFT), BF16),
            pltpu.VMEM((2, 3, 16, FFT + TAIL), BF16),
            pltpu.VMEM((2, 3, 16, FFT), BF16),
            pltpu.SemaphoreType.DMA((17,)),
            pltpu.SemaphoreType.DMA((copies,)),
            pltpu.SemaphoreType.DMA((copies,)),
        ],
        compiler_params=pltpu.CompilerParams(
            collective_id=0, has_side_effects=True, vmem_limit_bytes=63 << 20
        ),
    )(
        queries,
        new_latent,
        latent_cache.T,
        tables.T,
        context_len.reshape(1, REQS),
        group_rows.reshape(1, GRPS),
        request_order.reshape(1, REQS),
        jnp.swapaxes(residual, 1, 2),
        norm_gain,
        value_up,
        out_proj.T,
        gate_proj,
        up_proj,
        down_proj.T,
    )


def solution(mesh):
    placed = (
        P(None, "grp", "tp", None),
        P(None, "grp", None),
        P("grp", None),
        P("grp", None),
        P(),
        P(),
        P(),
        P(None, None, "grp"),
        P("tp", None, None),
        P("tp", "grp"),
        P("grp"),
        P("grp", "tp"),
        P("grp", "tp"),
        P("tp", "grp"),
    )
    return jax.shard_map(
        layer, mesh=mesh, in_specs=placed, out_specs=P(None, "tp", "grp"), check_vma=False
    )
```
